256 devices in a mesh: ctx: 64 (over y, x_lo, z), tp: 4 (over x_hi, core).
Axes of the slice: x: 4 (x_hi: 2, x_lo: 2; x = x_hi * 2 + x_lo), y: 4, z: 8, core: 2. Of those that a mesh axis runs over, the one named last changes fastest.
Arguments:
- tokens: bfloat16 [32768, 4096], P(('ctx', 'tp')), may hold values from -20 to 20
- norm_gain: float32 [4096], replicated, may hold values from 0.1 to 1.9
- w_query: bfloat16 [4096, 4096], P('ctx', 'tp'), may hold values from -1 to 1
- w_key: bfloat16 [4096, 512], P('ctx', 'tp'), may hold values from -16 to 16
- w_value: bfloat16 [4096, 512], P('ctx', 'tp'), may hold values from -0.09375 to 0.09375
- w_out: bfloat16 [4096, 4096], P('tp', 'ctx'), may hold values from -0.375 to 0.375
- doc_blocks: int32 [256], replicated, may hold values from 0 to 35, never falling along the last dimension, each value on 1 to 12 neighbouring positions
Outputs:
- attention_out: bfloat16 [32768, 4096], P(('ctx', 'tp'))
The draws below stay inside these ranges and needn't reach their ends.
Inputs may be any that keep to these rules, and one draw needn't show every extreme that they name: doc_blocks never falls; every document spans 1 to 12 blocks, and one spans exactly 12.
All inputs are finite; a program needn't handle non-finite values.
Results may differ from the reference program's by a relative error of at most 0.019.
Values may be sent and summed in bfloat16 or wider, within the bound.
A program may use at most 128 MiB of HBM per device.

```python
import math
import jax
import jax.numpy as jnp
import numpy as np
from jax import lax

D = 4096
HEADS = 32
KV_HEADS = 4
HD = 128
BLOCK = 128
SPAN = 4
TOK_CTX = 512
TOKENS = 32768
NBLK = 256
MOSTBLK = 12
DOCS = 36
N_CTX = 64
N_TP = 4


def shared_query(key):
    return jax.random.normal(key, (D, HEADS * HD), jnp.float32) * D ** (-0.5)


def draw_w_query(key, part):
    base_weight = shared_query(key)
    return base_weight.astype(jnp.bfloat16)


def draw_w_key(key, part):
    key = jax.random.fold_in(key, 12)
    own_weight = jax.random.normal(key, (D, KV_HEADS * HD), jnp.float32) * D ** (-0.5)
    return jnp.clip(own_weight, -16.0, 16.0).astype(jnp.bfloat16)


def draw_tokens(key, part):
    key = jax.random.fold_in(key, 13)
    key_base, key_rows, key_cols = jax.random.split(key, 3)
    row_scale = jnp.exp(jax.random.uniform(key_rows, (TOKENS, 1), jnp.float32, math.log(0.3), math.log(3.0)))
    col_scale = jnp.exp(jax.random.uniform(key_cols, (1, D), jnp.float32, math.log(0.5), math.log(2.0)))
    base_value = jax.random.normal(key_base, (TOKENS, D), jnp.float32)
    return jnp.clip(base_value * row_scale * col_scale, -20.0, 20.0).astype(jnp.bfloat16)


def block_levels(own_key, dims, cuts, low, top_value):
    factor_of, own = 1.0, jax.random.fold_in(own_key, 6)
    for position, blocks in cuts:
        heights = jnp.exp(jax.random.uniform(jax.random.fold_in(own, position), (blocks,), jnp.float32, low / len(cuts), top_value / len(cuts)))
        factor_of = factor_of * jnp.repeat(heights, dims[position] // blocks).reshape([-1 if axis == position else 1 for axis in range(len(dims))])
    return factor_of


def split_up(count, total, bound, skew):
    portions = [(1 << 20) // math.isqrt(rank ** skew) + 1 for rank in range(2, count + 1)]
    surplus, given = total - bound - (count - 1), [1] * (count - 1)
    while surplus > 0:
        free = [i for i in range(count - 1) if given[i] < bound]
        mass, left = sum([portions[i] for i in free]), surplus
        for i in free:
            extra = min(bound - given[i], max(1, left * portions[i] // mass), surplus)
            given[i] = given[i] + extra
            surplus = surplus - extra
    return np.array([bound] + given)


def ragged_sizes(stream_key, number_of, total, reach, lean):
    if number_of == 2:
        one = jax.random.randint(stream_key, (), max(1, total - reach), min(reach, total - 1) + 1)
        return jnp.stack([one, total - one])
    tallies = jnp.asarray(split_up(number_of, total, reach, lean), jnp.int32)
    couples = (number_of - 1) // 2
    donor, receiver = tallies[1:1 + 2 * couples:2], tallies[2:2 + 2 * couples:2]
    margin = jnp.minimum(donor - 1, reach - receiver)
    moved = jax.random.randint(jax.random.fold_in(stream_key, 1), (couples,), 0, 1 << 20) % (margin + 1)
    tallies = tallies.at[1:1 + 2 * couples:2].set(donor - moved).at[2:2 + 2 * couples:2].set(receiver + moved)
    return tallies[jax.random.permutation(jax.random.fold_in(stream_key, 2), number_of)]


def scatter_about(own_key, extent, scale, reach, cuts=(), held_as=jnp.bfloat16):
    drawn = jax.random.normal(own_key, extent, jnp.float32) * scale
    if len(cuts) > 0:
        drawn = block_levels(own_key, extent, cuts, -0.22, 0.18) * drawn
    return jnp.clip(drawn, min=-reach, max=reach).astype(held_as)


def setup_inputs(seed: int = 0) -> dict:
    key_of = jax.random.split(jax.random.key(seed), 8)
    tokens = draw_tokens(jax.random.fold_in(key_of[7], 71), 0)
    norm_gain = jnp.clip(1.0 + 0.18 * jax.random.normal(key_of[1], (D,), jnp.float32), 0.1, 1.9)
    w_query = draw_w_query(jax.random.fold_in(key_of[7], 71), 0)
    w_key = draw_w_key(jax.random.fold_in(key_of[7], 71), 0)
    w_value = scatter_about(key_of[4], (D, KV_HEADS * HD), D ** -0.5, 0.09375, ((0, 64), (1, 4)))
    w_out = scatter_about(key_of[5], (HEADS * HD, D), (HEADS * HD // 16) ** -0.5, 0.375, ((0, 4), (1, 64)))
    doc_blocks = jnp.searchsorted(jnp.cumsum(ragged_sizes(key_of[6], DOCS, NBLK, MOSTBLK, 2)), jnp.arange(NBLK), side="right").astype(jnp.int32)
    return {"tokens": tokens, "norm_gain": norm_gain, "w_query": w_query, "w_key": w_key, "w_value": w_value, "w_out": w_out, "doc_blocks": doc_blocks}


rope_base = 500000.0
neg_large = -1e+30

def rotate(values, positions):
    half_width = values.shape[-1] // 2
    frequency = rope_base ** (-jnp.arange(half_width, dtype=jnp.float32) / half_width)
    angles = positions.astype(jnp.float32)[:, None] * frequency[None, :]
    cosine = jnp.cos(angles)[:, None, :]
    sine_part = jnp.sin(angles)[:, None, :]
    first_half = values[..., :half_width]
    second_half = values[..., half_width:]
    return jnp.concatenate([first_half * cosine - second_half * sine_part, second_half * cosine + first_half * sine_part], axis=-1)

def reference(tokens, norm_gain, w_query, w_key, w_value, w_out, doc_blocks):
    token_float = tokens.astype(jnp.float32)
    scale_inv = lax.rsqrt(lax.optimization_barrier(jnp.mean(token_float * token_float, axis=-1, keepdims=True)) + 1e-05)
    normed = (token_float * scale_inv * norm_gain).astype(jnp.bfloat16)
    query_sum = jnp.dot(normed, w_query, preferred_element_type=jnp.float32)
    key_sum = jnp.dot(normed, w_key, preferred_element_type=jnp.float32)
    value_sum = jnp.dot(normed, w_value, preferred_element_type=jnp.float32)
    positions = jnp.arange(TOKENS, dtype=jnp.int32)
    group_size = HEADS // KV_HEADS
    query_heads = (rotate(query_sum.reshape(TOKENS, HEADS, HD), positions) * HD ** (-0.5)).astype(jnp.bfloat16)
    query_heads = query_heads.reshape(TOKENS, KV_HEADS, group_size, HD)
    key_heads = rotate(key_sum.reshape(TOKENS, KV_HEADS, HD), positions).astype(jnp.bfloat16)
    value_heads = value_sum.reshape(TOKENS, KV_HEADS, HD).astype(jnp.bfloat16)
    lead_rows = (SPAN - 1) * TOK_CTX
    key_padded = jnp.concatenate([jnp.zeros((lead_rows, KV_HEADS, HD), jnp.bfloat16), key_heads], axis=0)
    value_padded = jnp.concatenate([jnp.zeros((lead_rows, KV_HEADS, HD), jnp.bfloat16), value_heads], axis=0)
    token_docs = jnp.repeat(doc_blocks, BLOCK, total_repeat_length=TOKENS)
    docs_padded = jnp.concatenate([jnp.full((lead_rows,), -1, jnp.int32), token_docs])

    def one_block(block_index):
        query_start = (block_index * TOK_CTX).astype(jnp.int32)
        query_part = lax.dynamic_slice_in_dim(query_heads, query_start, TOK_CTX, 0).astype(jnp.float32)
        key_part = lax.dynamic_slice_in_dim(key_padded, query_start, SPAN * TOK_CTX, 0).astype(jnp.float32)
        value_part = lax.dynamic_slice_in_dim(value_padded, query_start, SPAN * TOK_CTX, 0).astype(jnp.float32)
        query_docs = lax.dynamic_slice_in_dim(token_docs, query_start, TOK_CTX, 0)
        key_docs = lax.dynamic_slice_in_dim(docs_padded, query_start, SPAN * TOK_CTX, 0)
        query_pos = query_start + jnp.arange(TOK_CTX, dtype=jnp.int32)
        key_pos = query_start - lead_rows + jnp.arange(SPAN * TOK_CTX, dtype=jnp.int32)
        visible = (query_docs[:, None] == key_docs[None, :]) & (key_pos[None, :] <= query_pos[:, None])
        visible = visible[:, None, None, :]
        scores = jnp.einsum('qkgd,skd->qkgs', query_part, key_part)
        scores = jnp.where(visible, scores, neg_large)
        top_score = lax.optimization_barrier(jnp.max(scores, axis=-1, keepdims=True))
        weights = jnp.where(visible, jnp.exp(scores - top_score), 0.0).astype(jnp.bfloat16)
        weight_sum = lax.optimization_barrier(jnp.sum(weights.astype(jnp.float32), axis=-1))
        summed = jnp.einsum('qkgs,skd->qkgd', weights.astype(jnp.float32), value_part)
        return (summed / weight_sum[..., None]).reshape(TOK_CTX, HEADS * HD).astype(jnp.bfloat16)
    attended = lax.map(one_block, jnp.arange(N_CTX, dtype=jnp.int32)).reshape(TOKENS, HEADS * HD)
    group_cols = HEADS * HD // N_TP
    total = jnp.zeros((TOKENS, D), jnp.float32)
    for group_index in range(N_TP):
        lower = group_index * group_cols
        product = jnp.dot(attended[:, lower:lower + group_cols], w_out[lower:lower + group_cols], preferred_element_type=jnp.float32)
        rounded = lax.optimization_barrier(product.astype(jnp.bfloat16)).astype(jnp.float32)
        total = total + rounded
    return total.astype(jnp.bfloat16)
```

```python
import functools

import jax
import jax.numpy as jnp
from jax import lax
from jax.experimental import pallas as pl
from jax.experimental.pallas import tpu as pltpu
from jax.sharding import PartitionSpec as P

HD = 128
BLOCK = 128
SPAN = 4
NY, NX, NZ = 4, 2, 8
MESH = pl.DeviceIdType.MESH

rope_base = 500000.0
neg_large = -1e30

Z_OFFSETS = [0, -1, 1, -2, 2, -3, 3, 4]
Y_OFFSETS = [0, -1, 1, 2]
COPIES_A = 1 + 8 + 32
COPIES_B = 1 + 4 + 32


def place():
    c = lax.axis_index("ctx")
    return c // (NX * NZ), lax.rem(c // NZ, NX), lax.rem(c, NZ)


def ctx_of(y, x, z):
    return (lax.rem(y + NY, NY) * NX + x) * NZ + lax.rem(z + NZ, NZ)


class Gather:
    def __init__(self, buf, send_sems, recv_sems, first, z_first):
        self.buf, self.send_sems, self.recv_sems = buf, send_sems, recv_sems
        self.y, self.x, self.z = place()
        self.first, self.z_first = first, z_first
        self.sent = []

    def copy(self, index, yy, zz, half, to):
        yy, zz = lax.rem(yy + 2 * NY, NY), lax.rem(zz + 2 * NZ, NZ)
        if half is None:
            ref = self.buf.at[yy, :, zz]
        else:
            ref = self.buf.at[yy, half, zz]
        return pltpu.make_async_remote_copy(
            src_ref=ref,
            dst_ref=ref,
            send_sem=self.send_sems.at[self.first + index],
            recv_sem=self.recv_sems.at[self.first + index],
            device_id={"ctx": ctx_of(*to)},
            device_id_type=MESH,
        )

    def ring_id(self, second, block, direction, hop, length):
        half_way = length // 2
        base = 1 if not second else 1 + 2 * (NZ if self.z_first else NY) // 2 + block * length
        return base + (0 if direction > 0 else half_way) + hop - 1

    def ring_copy(self, second, block, direction, hop):
        raise NotImplementedError

    def along_z(self, second, y_offset, block, direction, hop, sending):
        distance = hop - 1 if sending else hop
        half = (0 if direction > 0 else 1) if hop == NZ // 2 else None
        return self.copy(
            self.ring_id(second, block, direction, hop, NZ),
            self.y + y_offset,
            self.z - direction * distance,
            half,
            (self.y, self.x, self.z + direction),
        )

    def along_y(self, second, z_offset, block, direction, hop, sending):
        distance = hop - 1 if sending else hop
        half = (0 if direction > 0 else 1) if hop == NY // 2 else None
        return self.copy(
            self.ring_id(second, block, direction, hop, NY),
            self.y - direction * distance,
            self.z + z_offset,
            half,
            (self.y + direction, self.x, self.z),
        )

    def send(self, copy):
        copy.start()
        self.sent.append(copy)

    def first_ring(self, direction, hop, sending):
        if self.z_first:
            return self.along_z(False, 0, 0, direction, hop, sending)
        return self.along_y(False, 0, 0, direction, hop, sending)

    def second_ring(self, block, direction, hop, sending):
        if self.z_first:
            return self.along_y(True, Z_OFFSETS[block], block, direction, hop, sending)
        return self.along_z(True, Y_OFFSETS[block], block, direction, hop, sending)

    def exchange(self):
        copy = self.copy(0, self.y, self.z, self.x, (self.y, 1 - self.x, self.z))
        self.send(copy)

    def begin(self):
        self.copy(0, self.y, self.z, 1 - self.x, (self.y, 1 - self.x, self.z)).wait_recv()
        for direction in (1, -1):
            self.send(self.first_ring(direction, 1, True))
        for direction in (1, -1):
            self.send(self.second_ring(0, direction, 1, True))

    def first_arrival(self, hop):
        half_way = (NZ if self.z_first else NY) // 2
        for turn, direction in enumerate((1, -1)):
            self.first_ring(direction, hop, False).wait_recv()
            if hop < half_way:
                self.send(self.first_ring(direction, hop + 1, True))
                for across in (1, -1):
                    self.send(self.second_ring(2 * hop - 1 + turn, across, 1, True))
        if hop == half_way:
            for across in (1, -1):
                self.send(self.second_ring(2 * hop - 1, across, 1, True))

    def second_arrival(self, block, hop):
        half_way = (NY if self.z_first else NZ) // 2
        for direction in (1, -1):
            self.second_ring(block, direction, hop, False).wait_recv()
            if hop < half_way:
                self.send(self.second_ring(block, direction, hop + 1, True))

    def stages(self):
        blocks, ring, across = (NZ, NZ, NY) if self.z_first else (NY, NY, NZ)
        out = [[self.begin]]
        for hop in range(1, ring // 2 + 1):
            out.append([functools.partial(self.first_arrival, hop)])
        born = [0] + [(b + 1) // 2 for b in range(1, blocks)]
        pace = 2 if self.z_first else 4
        for b in range(blocks):
            for hop in range(1, across // 2 + 1):
                at = max(born[b] + hop, b * across * 3 // 2 // (2 * pace) + hop)
                while len(out) <= at:
                    out.append([])
                out[at].append(functools.partial(self.second_arrival, b, hop))
        return out

    def finish(self):
        for copy in self.sent:
            copy.wait_send()


def enter():
    y, x, z = place()
    barrier = pltpu.get_barrier_semaphore()
    to = [(y, 1 - x, z), (y + 1, x, z), (y - 1, x, z), (y, x, z + 1), (y, x, z - 1)]
    for t in to:
        pl.semaphore_signal(barrier, inc=1, device_id={"ctx": ctx_of(*t)}, device_id_type=MESH)
    pl.semaphore_wait(barrier, len(to))


Q_A, O_A = 768, 640


def gather_kernel(wq, wk, wv, wo, qa, qb, oa, ob, send_sems, recv_sems):
    y, x, z = place()
    qa[y, x, z] = wq[:, :Q_A]
    rest = wq.shape[1] - Q_A
    qb[y, x, z, :, :rest] = wq[:, Q_A:]
    qb[y, x, z, :, rest : rest + HD] = wk[...]
    qb[y, x, z, :, rest + HD :] = wv[...]
    oa[y, x, z] = wo[:, :O_A]
    ob[y, x, z] = wo[:, O_A:]
    enter()
    parts = []
    first = 0
    for buf, z_first in ((qa, True), (qb, False), (oa, True), (ob, False)):
        parts.append(Gather(buf, send_sems, recv_sems, first, z_first))
        first += COPIES_A if z_first else COPIES_B
    for part in parts:
        part.exchange()
    plans = [part.stages() for part in parts]
    lag = 5
    for stage in range(lag + max(len(plan) for plan in plans)):
        for index, plan in enumerate(plans):
            at = stage - (lag if index >= 2 else 0)
            if 0 <= at < len(plan):
                for step in plan[at]:
                    step()
    for part in parts:
        part.finish()


def gather_weights(w_query, w_key, w_value, w_out_t):
    rows = w_query.shape[0]
    widths = [Q_A, w_query.shape[1] - Q_A + 2 * HD, O_A, w_out_t.shape[1] - O_A]
    copies = 2 * (COPIES_A + COPIES_B)
    return pl.pallas_call(
        gather_kernel,
        out_shape=[jax.ShapeDtypeStruct((NY, NX, NZ, rows, w), jnp.bfloat16) for w in widths],
        in_specs=[pl.BlockSpec(memory_space=pltpu.VMEM)] * 4,
        out_specs=[pl.BlockSpec(memory_space=pltpu.VMEM)] * 4,
        scratch_shapes=[pltpu.SemaphoreType.DMA((copies,)), pltpu.SemaphoreType.DMA((copies,))],
        compiler_params=pltpu.CompilerParams(
            collective_id=0, has_side_effects=True, vmem_limit_bytes=48 * 1024 * 1024
        ),
    )(w_query, w_key, w_value, w_out_t)


def passed_along(value, axis, steps):
    count = lax.axis_size(axis)
    leading, last = (max(0, -steps), min(count, count - steps))
    return lax.ppermute(value, axis, [(source, source + steps) for source in range(leading, last)])


def rotate(values, positions):
    half_width = values.shape[-1] // 2
    frequency = rope_base ** (-jnp.arange(half_width, dtype=jnp.float32) / half_width)
    angles = positions.astype(jnp.float32)[:, None] * frequency[None, :]
    cosine = jnp.cos(angles)[:, None, :]
    sine_part = jnp.sin(angles)[:, None, :]
    first_half = values[..., :half_width]
    second_half = values[..., half_width:]
    return jnp.concatenate(
        [
            first_half * cosine - second_half * sine_part,
            second_half * cosine + first_half * sine_part,
        ],
        axis=-1,
    )


def doc_ranks(doc_blocks, source, per_device):
    start_block = jnp.maximum(source, 0) * per_device
    block_docs = lax.dynamic_slice_in_dim(doc_blocks, start_block, per_device, 0)
    block_docs = jnp.where(source >= 0, block_docs, -1)
    return jnp.repeat(block_docs, BLOCK, total_repeat_length=per_device * BLOCK)


def attend(attn_state, query_heads, key_block, value_block, query_docs, key_docs, causal):
    running_max, running_sum, running_out = attn_state
    scores = jnp.einsum(
        "qkgd,skd->qkgs", query_heads, key_block, preferred_element_type=jnp.float32
    )
    visible = query_docs[:, None] == key_docs[None, :]
    if causal is not None:
        visible = visible & causal
    visible = visible[:, None, None, :]
    scores = jnp.where(visible, scores, neg_large)
    new_max = jnp.maximum(running_max, jnp.max(scores, axis=-1))
    factor = jnp.exp(running_max - new_max)
    weights = jnp.where(visible, jnp.exp(scores - new_max[..., None]), 0.0).astype(jnp.bfloat16)
    new_sum = running_sum * factor + jnp.sum(weights, axis=-1, dtype=jnp.float32)
    new_out = running_out * factor[..., None] + jnp.einsum(
        "qkgs,skd->qkgd", weights, value_block, preferred_element_type=jnp.float32
    )
    return (new_max, new_sum, new_out)


def local(tokens, norm_gain, w_query, w_key, w_value, w_out, doc_blocks):
    ctx_index = lax.axis_index("ctx")
    token_float = tokens.astype(jnp.float32)
    scale_inv = lax.rsqrt(jnp.mean(token_float * token_float, axis=-1, keepdims=True) + 1e-05)
    normed = (token_float * scale_inv * norm_gain).astype(jnp.bfloat16)
    context_rows = lax.all_gather(normed, "tp", axis=0, tiled=True)
    row_count = context_rows.shape[0]
    qa, qb, oa, ob = gather_weights(w_query, w_key, w_value, w_out.T)
    sums = [
        jnp.dot(
            context_rows,
            w.reshape(-1, w.shape[-1]),
            preferred_element_type=jnp.float32,
        )
        for w in (qa, qb)
    ]
    rest = w_query.shape[1] - Q_A
    query_sum = jnp.concatenate([sums[0], sums[1][:, :rest]], axis=1)
    key_sum = sums[1][:, rest : rest + HD]
    value_sum = sums[1][:, rest + HD :]
    kv_local = w_key.shape[1] // HD
    group_size = w_query.shape[1] // w_key.shape[1]
    positions = ctx_index * row_count + jnp.arange(row_count, dtype=jnp.int32)
    query_heads = (
        rotate(query_sum.reshape(row_count, kv_local * group_size, HD), positions) * HD ** (-0.5)
    ).astype(jnp.bfloat16)
    query_heads = query_heads.reshape(row_count, kv_local, group_size, HD)
    key_heads = rotate(key_sum.reshape(row_count, kv_local, HD), positions).astype(jnp.bfloat16)
    value_heads = value_sum.reshape(row_count, kv_local, HD).astype(jnp.bfloat16)
    kv_local_pair = jnp.stack([key_heads, value_heads])
    per_device = row_count // BLOCK
    query_docs = doc_ranks(doc_blocks, ctx_index, per_device)
    row_iota = jnp.arange(row_count, dtype=jnp.int32)
    causal = row_iota[:, None] >= row_iota[None, :]
    init_state = (
        jnp.full((row_count, kv_local, group_size), neg_large, jnp.float32),
        jnp.zeros((row_count, kv_local, group_size), jnp.float32),
        jnp.zeros((row_count, kv_local, group_size, HD), jnp.float32),
    )
    attn_state = attend(
        init_state, query_heads, key_heads, value_heads, query_docs, query_docs, causal
    )

    def remote(current_state, distance, kv_block):
        key_docs = doc_ranks(doc_blocks, ctx_index - distance, per_device)
        return attend(
            current_state, query_heads, kv_block[0], kv_block[1], query_docs, key_docs, None
        )

    def relay_turn(turn_index, loop_carry):
        current_state, moving = loop_carry
        moving = passed_along(moving, "ctx", 1)
        return (remote(current_state, turn_index + 1, moving), moving)

    attn_state, moving = lax.fori_loop(0, SPAN - 1, relay_turn, (attn_state, kv_local_pair))
    final_max, final_sum, final_out = attn_state
    attended = (
        (final_out / final_sum[..., None])
        .reshape(row_count, kv_local * group_size * HD)
        .astype(jnp.bfloat16)
    )
    contract = (((1,), (1,)), ((), ()))
    partial_out = lax.dot_general(
        attended[:, :O_A], oa.reshape(-1, oa.shape[-1]), contract, preferred_element_type=jnp.float32
    ) + lax.dot_general(
        attended[:, O_A:], ob.reshape(-1, ob.shape[-1]), contract, preferred_element_type=jnp.float32
    )
    summed = lax.psum_scatter(
        partial_out.astype(jnp.bfloat16), "tp", scatter_dimension=0, tiled=True
    )
    return summed


def solution(mesh):
    return jax.shard_map(
        local,
        mesh=mesh,
        in_specs=(
            P(("ctx", "tp"), None),
            P(),
            P("ctx", "tp"),
            P("ctx", "tp"),
            P("ctx", "tp"),
            P("tp", "ctx"),
            P(),
        ),
        out_specs=P(("ctx", "tp"), None),
        check_vma=False,
    )
```

```python
import functools

import jax
import jax.numpy as jnp
from jax import lax
from jax.experimental import pallas as pl
from jax.experimental.pallas import tpu as pltpu
from jax.sharding import PartitionSpec as P

HD = 128
BLOCK = 128
WINDOW = 12
SPAN = 4
NY, NX, NZ, NTP = 4, 2, 8, 4
RING_X = 4
MESH = pl.DeviceIdType.MESH

rope_base = 500000.0
neg_large = -1e30

Z_OFFSETS = [0, -1, 1, -2, 2, -3, 3, 4]
Y_OFFSETS = [0, -1, 1, 2]
COPIES_A = 8 + 32
COPIES_B = 4 + 32
Q_A = 384
O_A = 384
NT = (((1,), (1,)), ((), ()))


class Place:
    def __init__(self):
        c, t = lax.axis_index("ctx"), lax.axis_index("tp")
        self.y, self.xl, self.z = c // (NX * NZ), lax.rem(c // NZ, NX), lax.rem(c, NZ)
        self.xh, self.core = t // 2, lax.rem(t, 2)
        self.x = self.xh * 2 + self.xl


def device(y, x, z, core):
    x = lax.rem(x + RING_X, RING_X)
    ctx = (lax.rem(y + NY, NY) * NX + lax.rem(x, 2)) * NZ + lax.rem(z + NZ, NZ)
    return (ctx, (x // 2) * 2 + core)


class Copies:
    def __init__(self, send_sems, recv_sems):
        self.send_sems, self.recv_sems = send_sems, recv_sems
        self.used = 0
        self.sent = []

    def reserve(self, count):
        first = self.used
        self.used += count
        return first

    def make(self, index, src, dst, to, recv_index=None):
        return pltpu.make_async_remote_copy(
            src_ref=src,
            dst_ref=dst,
            send_sem=self.send_sems.at[index],
            recv_sem=self.recv_sems.at[index if recv_index is None else recv_index],
            device_id=to,
            device_id_type=MESH,
        )

    def send(self, copy, when=None):
        if when is None:
            copy.start()
        else:
            pl.when(when)(copy.start)
        self.sent.append((copy, when))

    def finish(self):
        for copy, when in self.sent:
            if when is None:
                copy.wait_send()
            else:
                pl.when(when)(copy.wait_send)


class Gather:
    def __init__(self, here, copies, buf, z_first):
        self.here, self.copies, self.buf, self.z_first = here, copies, buf, z_first
        self.first = copies.reserve(COPIES_A if z_first else COPIES_B)
        self.arrive = copies.reserve(2)

    def exchange(self, parts):
        h = self.here
        for p in (0, 1):
            local = jnp.logical_and(h.core == h.xl, h.core == p)

            @pl.when(local)
            def _():
                self.buf[h.y, h.xl, h.z] = parts[p][...]

            copy = self.copies.make(
                self.arrive + p,
                parts[p],
                self.buf.at[h.y, h.xl, h.z],
                device(h.y, h.xh * 2 + h.core, h.z, p),
                self.arrive + h.xl,
            )
            self.copies.send(copy, jnp.logical_not(local))

    def exchanged(self):
        h = self.here
        for slot in (0, 1):
            local = jnp.logical_and(h.core == h.xl, h.xl == slot)
            ref = self.buf.at[h.y, slot, h.z]
            copy = self.copies.make(self.arrive + slot, ref, ref, device(h.y, h.x + 1, h.z, h.core))
            pl.when(jnp.logical_not(local))(copy.wait_recv)

    def copy(self, index, yy, zz, half, to):
        yy, zz = lax.rem(yy + 2 * NY, NY), lax.rem(zz + 2 * NZ, NZ)
        ref = self.buf.at[yy, :, zz] if half is None else self.buf.at[yy, half, zz]
        return self.copies.make(self.first + index, ref, ref, to)

    def ring_id(self, second, block, direction, hop, length):
        base = 0 if not second else (NZ if self.z_first else NY) + block * length
        return base + (0 if direction > 0 else length // 2) + hop - 1

    def along_z(self, second, y_offset, block, direction, hop, sending):
        h = self.here
        distance = hop - 1 if sending else hop
        half = (0 if direction > 0 else 1) if hop == NZ // 2 else None
        return self.copy(
            self.ring_id(second, block, direction, hop, NZ),
            h.y + y_offset,
            h.z - direction * distance,
            half,
            device(h.y, h.x, h.z + direction, h.core),
        )

    def along_y(self, second, z_offset, block, direction, hop, sending):
        h = self.here
        distance = hop - 1 if sending else hop
        half = (0 if direction > 0 else 1) if hop == NY // 2 else None
        return self.copy(
            self.ring_id(second, block, direction, hop, NY),
            h.y - direction * distance,
            h.z + z_offset,
            half,
            device(h.y + direction, h.x, h.z, h.core),
        )

    def first_ring(self, direction, hop, sending):
        along = self.along_z if self.z_first else self.along_y
        return along(False, 0, 0, direction, hop, sending)

    def second_ring(self, block, direction, hop, sending):
        if self.z_first:
            return self.along_y(True, Z_OFFSETS[block], block, direction, hop, sending)
        return self.along_z(True, Y_OFFSETS[block], block, direction, hop, sending)

    def begin(self):
        self.exchanged()
        for direction in (1, -1):
            self.copies.send(self.first_ring(direction, 1, True))
        for direction in (1, -1):
            self.copies.send(self.second_ring(0, direction, 1, True))

    def first_arrival(self, hop):
        half_way = (NZ if self.z_first else NY) // 2
        for turn, direction in enumerate((1, -1)):
            self.first_ring(direction, hop, False).wait_recv()
            if hop < half_way:
                self.copies.send(self.first_ring(direction, hop + 1, True))
                for across in (1, -1):
                    self.copies.send(self.second_ring(2 * hop - 1 + turn, across, 1, True))
        if hop == half_way:
            for across in (1, -1):
                self.copies.send(self.second_ring(2 * hop - 1, across, 1, True))

    def second_arrival(self, block, hop):
        half_way = (NY if self.z_first else NZ) // 2
        for direction in (1, -1):
            self.second_ring(block, direction, hop, False).wait_recv()
            if hop < half_way:
                self.copies.send(self.second_ring(block, direction, hop + 1, True))

    def stages(self):
        blocks, ring, across = (NZ, NZ, NY) if self.z_first else (NY, NY, NZ)
        out = [[self.begin]]
        for hop in range(1, ring // 2 + 1):
            out.append([functools.partial(self.first_arrival, hop)])
        born = [0] + [(b + 1) // 2 for b in range(1, blocks)]
        pace = 2 if self.z_first else 4
        for b in range(blocks):
            for hop in range(1, across // 2 + 1):
                at = max(born[b] + hop, b * across * 3 // 2 // (2 * pace) + hop)
                while len(out) <= at:
                    out.append([])
                out[at].append(functools.partial(self.second_arrival, b, hop))
        return out


class Tokens:
    def __init__(self, here, copies, rows):
        self.here, self.copies, self.rows = here, copies, rows
        self.first = copies.reserve(13)

    def part(self, x, core, half):
        x = lax.rem(x + RING_X, RING_X)
        ref = self.rows.at[lax.rem(x, 2), (x // 2) * 2 + core]
        return ref if half is None else ref.at[pl.ds(half * (BLOCK // 2), BLOCK // 2)]

    def ring(self, direction, hop, half, sending):
        h = self.here
        index = (0 if direction > 0 else 2) + half if hop == 1 else 4 + half
        ref = self.part(h.x - direction * (hop - 1 if sending else hop), h.core, half)
        return self.copies.make(self.first + index, ref, ref, device(h.y, h.x + direction, h.z, h.core))

    def beside(self, distance, half, sending):
        h = self.here
        index = 6 if half is None else {-1: 7, 1: 9, 2: 11}[distance] + half
        ref = self.part(h.x + distance, h.core if sending else 1 - h.core, half)
        return self.copies.make(self.first + index, ref, ref, device(h.y, h.x, h.z, 1 - h.core))

    def begin(self):
        for turn in (0, 1):
            self.copies.send(self.ring(1, 1, turn, True))
            self.copies.send(self.ring(-1, 1, 1 - turn, True))
        self.copies.send(self.beside(0, None, True))

    def first_hop(self, turn):
        for direction in (1, -1):
            half = turn if direction > 0 else 1 - turn
            self.ring(direction, 1, half, False).wait_recv()
            if turn == 0:
                self.copies.send(self.ring(direction, 2, half, True))
            self.copies.send(self.beside(-direction, half, True))

    def second_hop(self):
        for direction, half in ((1, 0), (-1, 1)):
            self.ring(direction, 2, half, False).wait_recv()
            self.copies.send(self.beside(2, half, True))

    def rest(self):
        self.beside(0, None, False).wait_recv()
        for distance in (-1, 1, 2):
            for half in (0, 1):
                self.beside(distance, half, False).wait_recv()


class Relay:
    def __init__(self, here, copies, kv, hops):
        self.here, self.copies, self.kv, self.hops = here, copies, kv, hops
        self.first = copies.reserve(10)

    def slot(self, kind, distance, xl=None):
        rows = pl.ds((SPAN - 1 - distance) * self.rows(), self.rows())
        return self.kv.at[kind, :, rows] if xl is None else self.kv.at[kind, xl, rows]

    def rows(self):
        return self.kv.shape[2] // SPAN

    def along(self, distance):
        h = self.here
        src = self.slot(h.core, 0) if distance == 1 else self.hops.at[distance - 2]
        return self.copies.make(
            self.first + distance - 1,
            src,
            self.hops.at[distance - 1],
            device(h.y, h.x, h.z + 1, h.core),
        )

    def over(self, distance):
        h = self.here
        return self.copies.make(
            self.first + 2 + distance,
            self.hops.at[distance - 1, 1],
            self.slot(h.core, distance, 0),
            device(h.y + 1, h.x, h.z, h.core),
        )

    def beside(self, distance, sending):
        h = self.here
        ref = self.slot(h.core if sending else 1 - h.core, distance)
        return self.copies.make(self.first + 6 + distance, ref, ref, device(h.y, h.x, h.z, 1 - h.core))

    def begin(self):
        self.copies.send(self.along(1))
        self.copies.send(self.beside(0, True))

    def arrival(self, distance):
        h = self.here
        self.along(distance).wait_recv()
        if distance < SPAN - 1:
            self.copies.send(self.along(distance + 1))
        wrapped = h.z < distance
        start = (SPAN - 1 - distance) * self.rows()
        rows = pl.ds(start, self.rows())
        self.copies.send(self.over(distance), wrapped)

        @pl.when(wrapped)
        def _():
            self.kv[h.core, 1, rows] = self.hops[distance - 1, 0]

        @pl.when(jnp.logical_not(wrapped))
        def _():
            self.kv[h.core, 0, rows] = self.hops[distance - 1, 0]
            self.kv[h.core, 1, rows] = self.hops[distance - 1, 1]

    def placed(self, distance):
        pl.when(self.here.z < distance)(self.over(distance).wait_recv)
        self.copies.send(self.beside(distance, True))

    def rest(self):
        for distance in range(SPAN):
            self.beside(distance, False).wait_recv()


class Products:
    def __init__(self, here, copies, own, other, part_a, part_b, whole_a, whole_b):
        self.here, self.copies, self.own, self.other = here, copies, own, other
        self.half_way = {1: part_a, -1: part_b}
        self.whole = {1: whole_a, -1: whole_b}
        self.first = copies.reserve(10)
        self.width = own.shape[-1] // 2

    def columns(self, half):
        return pl.ds(half * self.width, self.width)

    def beside(self, j):
        h = self.here
        return self.copies.make(
            self.first + j,
            self.own.at[1 - h.core, j],
            self.other.at[j],
            device(h.y, h.x, h.z, 1 - h.core),
        )

    def far(self, direction):
        h = self.here
        half = 0 if direction > 0 else 1
        return self.copies.make(
            self.first + 4 + half,
            self.own.at[h.core, 0, :, self.columns(half)],
            self.half_way[direction],
            device(h.y, h.x + direction, h.z, h.core),
        )

    def near(self, direction, half):
        h = self.here
        j = 1 if direction > 0 else 2
        return self.copies.make(
            self.first + 6 + 2 * (j - 1) + half,
            self.own.at[h.core, j, :, self.columns(half)],
            self.whole[direction].at[:, self.columns(half)],
            device(h.y, h.x + direction, h.z, h.core),
        )

    def add(self, j, half, more=None):
        h = self.here
        tile = 512

        def body(step, _):
            inner = pl.multiple_of(step * tile, tile)
            at = pl.ds(pl.multiple_of(half * self.width + inner, tile), tile)
            total = self.own[h.core, j, :, at].astype(jnp.float32) + self.other[j, :, at].astype(jnp.float32)
            if more is not None:
                total = total + more[:, pl.ds(inner, tile)].astype(jnp.float32)
            self.own[h.core, j, :, at] = total.astype(jnp.bfloat16)
            return 0

        lax.fori_loop(0, self.width // tile, body, 0)

    def reduce(self, j):
        self.beside(j).wait_recv()
        if j == 0:
            for direction in (1, -1):
                self.add(0, 0 if direction > 0 else 1)
                self.copies.send(self.far(direction))
        elif j < 3:
            direction = 1 if j == 1 else -1
            half = 1 if direction > 0 else 0
            self.add(j, half)
            self.copies.send(self.near(direction, half))

    def last(self, out):
        h = self.here
        for direction in (1, -1):
            j, half = (1, 0) if direction > 0 else (2, 1)
            self.far(direction).wait_recv()
            self.add(j, half, self.half_way[direction])
            self.copies.send(self.near(direction, half))
        for half in (0, 1):
            for direction in (1, -1):
                self.near(direction, half).wait_recv()
        tile = 512

        def body(step, _):
            at = pl.ds(pl.multiple_of(step * tile, tile), tile)
            total = self.own[h.core, 3, :, at].astype(jnp.float32) + self.other[3, :, at].astype(jnp.float32)
            for direction in (1, -1):
                total = total + self.whole[direction][:, at].astype(jnp.float32)
            out[:, at] = total.astype(out.dtype)
            return 0

        lax.fori_loop(0, 2 * self.width // tile, body, 0)


def neighbours(h):
    outer = h.x - 1 + 2 * h.xl
    return [
        device(h.y, h.x, h.z, 1 - h.core),
        device(h.y, h.xh * 2 + 1 - h.xl, h.z, h.core),
        device(h.y, h.xh * 2 + 1 - h.xl, h.z, 1 - h.core),
        device(h.y, outer, h.z, h.core),
        device(h.y + 1, h.x, h.z, h.core),
        device(h.y - 1, h.x, h.z, h.core),
        device(h.y, h.x, h.z + 1, h.core),
        device(h.y, h.x, h.z - 1, h.core),
    ]


def block_kernel(
    tokens, gain, wq, wk, wv, wo, cosine, sine, bias, out,
    rows, qa, qb, qb_own, oa, ob, queries, kv, values, hops, attended,
    own, other, part_a, part_b, whole_a, whole_b, send_sems, recv_sems,
):
    h = Place()
    half_heads = wq.shape[1] // 2
    barrier = pltpu.get_barrier_semaphore()
    greeted = neighbours(h)
    for to in greeted:
        pl.semaphore_signal(barrier, inc=1, device_id=to, device_id_type=MESH)

    for p, kind in ((0, wk), (1, wv)):
        qb_own[p, :, :HD] = wq[:, p * half_heads + Q_A : (p + 1) * half_heads]
        qb_own[p, :, HD:] = kind[...]

    def norm(step, _):
        at = pl.ds(pl.multiple_of(step * 32, 32), 32)
        value = tokens[at, :].astype(jnp.float32)
        scale = lax.rsqrt(jnp.mean(value * value, axis=-1, keepdims=True) + 1e-05)
        rows[h.xl, h.xh * 2 + h.core, at, :] = (value * scale * gain[...]).astype(jnp.bfloat16)
        return 0

    lax.fori_loop(0, BLOCK // 32, norm, 0)
    pl.semaphore_wait(barrier, len(greeted))

    copies = Copies(send_sems, recv_sems)
    gathers = [Gather(h, copies, buf, z_first) for buf, z_first in ((qa, True), (qb, False), (oa, True), (ob, False))]
    token_rows = Tokens(h, copies, rows)
    relay = Relay(h, copies, kv, hops)
    products = Products(h, copies, own, other, part_a, part_b, whole_a, whole_b)

    gathers[0].exchange([wq.at[:, pl.ds(p * half_heads, Q_A)] for p in (0, 1)])
    gathers[1].exchange([qb_own.at[p] for p in (0, 1)])
    token_rows.begin()
    gathers[2].exchange([wo.at[:, pl.ds(p * half_heads, O_A)] for p in (0, 1)])
    gathers[3].exchange([wo.at[:, pl.ds(p * half_heads + O_A, half_heads - O_A)] for p in (0, 1)])

    plans = [part.stages() for part in gathers]

    def run(which, stage):
        for index in which:
            if 0 <= stage < len(plans[index]):
                for step in plans[index][stage]:
                    step()

    first_stages = max(len(plans[0]), len(plans[1]))
    last_stages = max(len(plans[2]), len(plans[3]))
    early = 3
    for stage in range(first_stages):
        run((0, 1), stage)
        run((2, 3), stage - (first_stages - early))
        if stage == 4:
            token_rows.first_hop(0)
        if stage == first_stages - 2:
            token_rows.first_hop(1)
    token_rows.second_hop()
    token_rows.rest()

    def project(weights, chip):
        at = pl.ds((chip // 2) * 2, 2)
        total = None
        depth = NX * NZ * weights.shape[3]
        for y in range(NY):
            left = rows[lax.rem(chip, 2), at, :, y * depth : (y + 1) * depth].reshape(2 * BLOCK, depth)
            term = jnp.dot(left, weights[y].reshape(depth, weights.shape[4]), preferred_element_type=jnp.float32)
            total = term if total is None else total + term
        return total

    def rotated(value, chip):
        at = pl.ds(pl.multiple_of((chip // 2) * (2 * BLOCK), 2 * BLOCK), 2 * BLOCK)
        swapped = pltpu.roll(value, HD // 2, 1)
        return value * cosine[lax.rem(chip, 2), at, :] + swapped * sine[lax.rem(chip, 2), at, :]

    def keep_query(value, chip, head):
        query = (rotated(value, chip) * HD ** (-0.5)).astype(jnp.bfloat16)
        for core in (0, 1):
            queries[lax.rem(chip, 2), (chip // 2) * 2 + core, head * BLOCK : (head + 1) * BLOCK, :] = query[
                core * BLOCK : (core + 1) * BLOCK
            ]

    def project_b(chip, _):
        total = project(qb, chip)
        keep_query(total[:, :HD], chip, 3)
        value = total[:, HD:]
        value = jnp.where(h.core == 0, rotated(value, chip), value).astype(jnp.bfloat16)
        start = (SPAN - 1) * NTP * BLOCK + (chip // 2) * (2 * BLOCK)
        kv[h.core, lax.rem(chip, 2), pl.ds(pl.multiple_of(start, 2 * BLOCK), 2 * BLOCK), :] = value
        return 0

    def project_a(chip, _):
        total = project(qa, chip)
        for head in range(3):
            keep_query(total[:, head * HD : (head + 1) * HD], chip, head)
        return 0

    lax.fori_loop(0, RING_X, project_b, 0)
    relay.begin()
    run((2, 3), early)
    lax.fori_loop(0, RING_X, project_a, 0)
    stage = early + 1
    for distance in range(1, SPAN):
        relay.arrival(distance)
        run((2, 3), stage)
        stage += 1
        relay.placed(distance)
    for stage in range(stage, last_stages):
        run((2, 3), stage)
    relay.rest()

    values[:, :, HD:] = jnp.ones_like(values[:, :, HD:])
    for xl in range(NX):
        values[xl, :, :HD] = kv[1, xl]

    heads = half_heads // HD
    query_at = lax.broadcasted_iota(jnp.int32, (2 * BLOCK, BLOCK), 0)
    query_at = lax.rem(query_at, BLOCK)
    causal = jnp.where(query_at >= lax.broadcasted_iota(jnp.int32, (2 * BLOCK, BLOCK), 1), 0.0, neg_large)

    def attend(chip):
        xl, first_block = lax.rem(chip, 2), (chip // 2) * 2

        def body(step, _):
            block = first_block + step
            window = pl.ds(pl.multiple_of((block + SPAN * NTP - WINDOW - (NTP - 1)) * BLOCK, BLOCK), WINDOW * BLOCK)
            for pair in range(heads // 2):
                query = queries[xl, block, pair * 2 * BLOCK : (pair + 1) * 2 * BLOCK, :]
                scores = lax.dot_general(query, kv[0, xl, window, :], NT, preferred_element_type=jnp.float32)
                scores = scores + bias[xl * NTP + block]
                near = (WINDOW - 1) * BLOCK
                scores = jnp.concatenate([scores[:, :near], scores[:, near:] + causal], axis=1)
                top = jnp.max(scores, axis=-1, keepdims=True)
                weights = jnp.exp(scores - top).astype(jnp.bfloat16)
                total = jnp.dot(weights, values[xl, window, :], preferred_element_type=jnp.float32)
                result = (total[:, :HD] / total[:, HD:]).astype(jnp.bfloat16)
                for k in range(2):
                    head = pair * 2 + k
                    attended[xl, block, :, head * HD : (head + 1) * HD] = result[k * BLOCK : (k + 1) * BLOCK]
            return 0

        lax.fori_loop(0, 2, body, 0)

    def multiply(j, chip):
        xl, first_block = lax.rem(chip, 2), (chip // 2) * 2
        tile = NZ * wo.shape[0]

        def body(step, _):
            left = attended[xl, pl.ds(first_block, 2)].reshape(2 * BLOCK, half_heads)
            y, x = step // NX, lax.rem(step, NX)
            right = jnp.concatenate(
                [oa[y, x].reshape(tile, O_A), ob[y, x].reshape(tile, half_heads - O_A)], axis=1
            )
            total = lax.dot_general(left, right, NT, preferred_element_type=jnp.float32).astype(jnp.bfloat16)
            at = pl.ds(pl.multiple_of(step * tile, tile), tile)
            for core in (0, 1):
                own[core, j, :, at] = total[core * BLOCK : (core + 1) * BLOCK]
            return 0

        lax.fori_loop(0, NY * NX, body, 0)

    for j, offset in enumerate((2, 1, 3, 0)):
        chip = lax.rem(h.x + offset, RING_X)
        attend(chip)
        if j > 0:
            products.reduce(j - 1)
        multiply(j, chip)
        copies.send(products.beside(j))
    products.reduce(3)
    products.last(out)
    copies.finish()


COPIES = 2 * (COPIES_A + COPIES_B + 4) + 13 + 10 + 10


def whole_block(tokens, gain, w_query, w_key, w_value, w_out_t, cosine, sine, bias):
    count, width = tokens.shape
    rows = w_query.shape[0]
    half = w_query.shape[1] // 2
    near = NTP * count
    bf16 = jnp.bfloat16
    vmem = pl.BlockSpec(memory_space=pltpu.VMEM)
    return pl.pallas_call(
        block_kernel,
        out_shape=jax.ShapeDtypeStruct((count, width), bf16),
        in_specs=[vmem] * 9,
        out_specs=vmem,
        scratch_shapes=[
            pltpu.VMEM((NX, NTP, count, width), bf16),
            pltpu.VMEM((NY, NX, NZ, rows, Q_A), bf16),
            pltpu.VMEM((NY, NX, NZ, rows, half - Q_A + HD), bf16),
            pltpu.VMEM((2, rows, half - Q_A + HD), bf16),
            pltpu.VMEM((NY, NX, NZ, rows, O_A), bf16),
            pltpu.VMEM((NY, NX, NZ, rows, half - O_A), bf16),
            pltpu.VMEM((NX, NTP, half // HD * BLOCK, HD), bf16),
            pltpu.VMEM((2, NX, SPAN * near, HD), bf16),
            pltpu.VMEM((NX, SPAN * near, 2 * HD), bf16),
            pltpu.VMEM((SPAN - 1, NX, near, HD), bf16),
            pltpu.VMEM((NX, NTP, count, half), bf16),
            pltpu.VMEM((2, RING_X, count, width), bf16),
            pltpu.VMEM((RING_X, count, width), bf16),
            pltpu.VMEM((count, width // 2), bf16),
            pltpu.VMEM((count, width // 2), bf16),
            pltpu.VMEM((count, width), bf16),
            pltpu.VMEM((count, width), bf16),
            pltpu.SemaphoreType.DMA((COPIES,)),
            pltpu.SemaphoreType.DMA((COPIES,)),
        ],
        compiler_params=pltpu.CompilerParams(
            collective_id=0, has_side_effects=True, vmem_limit_bytes=60 * 1024 * 1024
        ),
    )(tokens, gain, w_query, w_key, w_value, w_out_t, cosine, sine, bias)


def tables(doc_blocks, count):
    c = lax.axis_index("ctx")
    y, z = c // (NX * NZ), lax.rem(c, NZ)
    contexts = y * (NX * NZ) + jnp.arange(NX, dtype=jnp.int32) * NZ + z
    positions = contexts[:, None] * (NTP * count) + jnp.arange(NTP * count, dtype=jnp.int32)[None, :]
    half_width = HD // 2
    frequency = rope_base ** (-jnp.arange(half_width, dtype=jnp.float32) / half_width)
    angles = positions.astype(jnp.float32)[..., None] * frequency
    cosine, sine = jnp.cos(angles), jnp.sin(angles)
    cosine = jnp.concatenate([cosine, cosine], axis=-1)
    sine = jnp.concatenate([-sine, sine], axis=-1)
    blocks = (contexts[:, None] * NTP + jnp.arange(NTP, dtype=jnp.int32)).reshape(-1)
    keys = blocks[:, None] - (WINDOW - 1) + jnp.arange(WINDOW, dtype=jnp.int32)
    visible = (keys >= 0) & (doc_blocks[jnp.maximum(keys, 0)] == doc_blocks[blocks][:, None])
    bias = jnp.where(visible, 0.0, neg_large).astype(jnp.float32)
    bias = jnp.broadcast_to(bias[:, None, :, None], (NX * NTP, 1, WINDOW, BLOCK)).reshape(NX * NTP, 1, WINDOW * BLOCK)
    return cosine, sine, bias


def local(tokens, norm_gain, w_query, w_key, w_value, w_out, doc_blocks):
    cosine, sine, bias = tables(doc_blocks, tokens.shape[0])
    return whole_block(tokens, norm_gain[None, :], w_query, w_key, w_value, w_out.T, cosine, sine, bias)


def solution(mesh):
    return jax.shard_map(
        local,
        mesh=mesh,
        in_specs=(
            P(("ctx", "tp"), None),
            P(),
            P("ctx", "tp"),
            P("ctx", "tp"),
            P("ctx", "tp"),
            P("tp", "ctx"),
            P(),
        ),
        out_specs=P(("ctx", "tp"), None),
        check_vma=False,
    )
```

```python
import functools

import jax
import jax.numpy as jnp
import numpy as np
from jax import lax
from jax.experimental import pallas as pl
from jax.experimental.pallas import tpu as pltpu
from jax.sharding import PartitionSpec as P

HD = 128
BLOCK = 128
WINDOW = 12
SPAN = 4
NY, NX, NZ, NTP = 4, 2, 8, 4
RING_X = 4
MESH = pl.DeviceIdType.MESH

rope_base = 500000.0
neg_large = -1e30

Z_OFFSETS = [0, -1, 1, -2, 2, -3, 3, 4]
Y_OFFSETS = [0, -1, 1, 2]
COPIES_A = 8 + 32
COPIES_B = 4 + 32
RELAY_COPIES = 17
PRODUCT_COPIES = 14
Q_A = 384
O_A = 384
NT = (((1,), (1,)), ((), ()))


class Place:
    def __init__(self):
        c, t = lax.axis_index("ctx"), lax.axis_index("tp")
        self.y, self.xl, self.z = c // (NX * NZ), lax.rem(c // NZ, NX), lax.rem(c, NZ)
        self.xh, self.core = t // 2, lax.rem(t, 2)
        self.x = self.xh * 2 + self.xl


def device(y, x, z, core):
    x = lax.rem(x + RING_X, RING_X)
    ctx = (lax.rem(y + NY, NY) * NX + lax.rem(x, 2)) * NZ + lax.rem(z + NZ, NZ)
    return (ctx, (x // 2) * 2 + core)


class Copies:
    def __init__(self, send_sems, recv_sems):
        self.send_sems, self.recv_sems = send_sems, recv_sems
        self.used = 0
        self.sent = []

    def reserve(self, count):
        first = self.used
        self.used += count
        return first

    def make(self, index, src, dst, to, recv_index=None):
        return pltpu.make_async_remote_copy(
            src_ref=src,
            dst_ref=dst,
            send_sem=self.send_sems.at[index],
            recv_sem=self.recv_sems.at[index if recv_index is None else recv_index],
            device_id=to,
            device_id_type=MESH,
        )

    def send(self, copy, when=None):
        if when is None:
            copy.start()
        else:
            pl.when(when)(copy.start)
        self.sent.append((copy, when))

    def finish(self):
        for copy, when in self.sent:
            if when is None:
                copy.wait_send()
            else:
                pl.when(when)(copy.wait_send)


class Gather:
    def __init__(self, here, copies, buf, z_first):
        self.here, self.copies, self.buf, self.z_first = here, copies, buf, z_first
        self.first = copies.reserve(COPIES_A if z_first else COPIES_B)
        self.arrive = copies.reserve(2)

    def exchange(self, parts):
        h = self.here
        for p in (0, 1):
            local = jnp.logical_and(h.core == h.xl, h.core == p)

            @pl.when(local)
            def _():
                self.buf[h.y, h.xl, h.z] = parts[p][...]

            copy = self.copies.make(
                self.arrive + p,
                parts[p],
                self.buf.at[h.y, h.xl, h.z],
                device(h.y, h.xh * 2 + h.core, h.z, p),
                self.arrive + h.xl,
            )
            self.copies.send(copy, jnp.logical_not(local))

    def exchanged(self):
        h = self.here
        for slot in (0, 1):
            local = jnp.logical_and(h.core == h.xl, h.xl == slot)
            ref = self.buf.at[h.y, slot, h.z]
            copy = self.copies.make(self.arrive + slot, ref, ref, device(h.y, h.x + 1, h.z, h.core))
            pl.when(jnp.logical_not(local))(copy.wait_recv)

    def copy(self, index, yy, zz, half, to):
        yy, zz = lax.rem(yy + 2 * NY, NY), lax.rem(zz + 2 * NZ, NZ)
        ref = self.buf.at[yy, :, zz] if half is None else self.buf.at[yy, half, zz]
        return self.copies.make(self.first + index, ref, ref, to)

    def ring_id(self, second, block, direction, hop, length):
        base = 0 if not second else (NZ if self.z_first else NY) + block * length
        return base + (0 if direction > 0 else length // 2) + hop - 1

    def along_z(self, second, y_offset, block, direction, hop, sending):
        h = self.here
        distance = hop - 1 if sending else hop
        half = (0 if direction > 0 else 1) if hop == NZ // 2 else None
        return self.copy(
            self.ring_id(second, block, direction, hop, NZ),
            h.y + y_offset,
            h.z - direction * distance,
            half,
            device(h.y, h.x, h.z + direction, h.core),
        )

    def along_y(self, second, z_offset, block, direction, hop, sending):
        h = self.here
        distance = hop - 1 if sending else hop
        half = (0 if direction > 0 else 1) if hop == NY // 2 else None
        return self.copy(
            self.ring_id(second, block, direction, hop, NY),
            h.y - direction * distance,
            h.z + z_offset,
            half,
            device(h.y + direction, h.x, h.z, h.core),
        )

    def first_ring(self, direction, hop, sending):
        along = self.along_z if self.z_first else self.along_y
        return along(False, 0, 0, direction, hop, sending)

    def second_ring(self, block, direction, hop, sending):
        if self.z_first:
            return self.along_y(True, Z_OFFSETS[block], block, direction, hop, sending)
        return self.along_z(True, Y_OFFSETS[block], block, direction, hop, sending)

    def begin(self):
        self.exchanged()
        for direction in (1, -1):
            self.copies.send(self.first_ring(direction, 1, True))
        for direction in (1, -1):
            self.copies.send(self.second_ring(0, direction, 1, True))

    def first_arrival(self, hop):
        half_way = (NZ if self.z_first else NY) // 2
        for turn, direction in enumerate((1, -1)):
            self.first_ring(direction, hop, False).wait_recv()
            if hop < half_way:
                self.copies.send(self.first_ring(direction, hop + 1, True))
                for across in (1, -1):
                    self.copies.send(self.second_ring(2 * hop - 1 + turn, across, 1, True))
        if hop == half_way:
            for across in (1, -1):
                self.copies.send(self.second_ring(2 * hop - 1, across, 1, True))

    def second_arrival(self, block, hop):
        half_way = (NY if self.z_first else NZ) // 2
        for direction in (1, -1):
            self.second_ring(block, direction, hop, False).wait_recv()
            if hop < half_way:
                self.copies.send(self.second_ring(block, direction, hop + 1, True))

    def stages(self):
        blocks, ring, across = (NZ, NZ, NY) if self.z_first else (NY, NY, NZ)
        out = [[self.begin]]
        for hop in range(1, ring // 2 + 1):
            out.append([functools.partial(self.first_arrival, hop)])
        for b in range(blocks):
            for hop in range(1, across // 2):
                at = (b + 1) // 2 + hop
                while len(out) <= at:
                    out.append([])
                out[at].append(functools.partial(self.second_arrival, b, hop))
        return out

    def rest(self):
        blocks, across = (NZ, NY) if self.z_first else (NY, NZ)
        for b in range(blocks):
            self.second_arrival(b, across // 2)


class Tokens:
    def __init__(self, here, copies, rows):
        self.here, self.copies, self.rows = here, copies, rows
        self.first = copies.reserve(13)

    def part(self, x, core, half):
        x = lax.rem(x + RING_X, RING_X)
        ref = self.rows.at[lax.rem(x, 2), (x // 2) * 2 + core]
        return ref if half is None else ref.at[pl.ds(half * (BLOCK // 2), BLOCK // 2)]

    def ring(self, direction, hop, half, sending):
        h = self.here
        index = (0 if direction > 0 else 2) + half if hop == 1 else 4 + half
        ref = self.part(h.x - direction * (hop - 1 if sending else hop), h.core, half)
        return self.copies.make(self.first + index, ref, ref, device(h.y, h.x + direction, h.z, h.core))

    def beside(self, distance, half, sending):
        h = self.here
        index = 6 if half is None else {-1: 7, 1: 9, 2: 11}[distance] + half
        ref = self.part(h.x + distance, h.core if sending else 1 - h.core, half)
        return self.copies.make(self.first + index, ref, ref, device(h.y, h.x, h.z, 1 - h.core))

    def begin(self):
        for turn in (0, 1):
            self.copies.send(self.ring(1, 1, turn, True))
            self.copies.send(self.ring(-1, 1, 1 - turn, True))
        self.copies.send(self.beside(0, None, True))

    def first_hop(self, turn):
        for direction in (1, -1):
            half = turn if direction > 0 else 1 - turn
            self.ring(direction, 1, half, False).wait_recv()
            if turn == 0:
                self.copies.send(self.ring(direction, 2, half, True))
            self.copies.send(self.beside(-direction, half, True))

    def second_hop(self):
        for direction, half in ((1, 0), (-1, 1)):
            self.ring(direction, 2, half, False).wait_recv()
            self.copies.send(self.beside(2, half, True))

    def rest(self):
        self.beside(0, None, False).wait_recv()
        for distance in (-1, 1, 2):
            for half in (0, 1):
                self.beside(distance, half, False).wait_recv()


class Relay:
    def __init__(self, here, copies, kv, hops):
        self.here, self.copies, self.kv, self.hops = here, copies, kv, hops
        self.first = copies.reserve(RELAY_COPIES)
        self.count = kv.shape[2] // SPAN

    def rows(self, distance, offset=0):
        skipped = BLOCK if distance == SPAN - 1 else 0
        return pl.ds(offset + skipped, self.count - skipped)

    def slot(self, kind, distance, xl):
        return self.kv.at[kind, xl, self.rows(distance, (SPAN - 1 - distance) * self.count)]

    def hop(self, distance, xl, needed=None):
        rows = self.rows(distance if needed is None else needed)
        return self.hops.at[distance - 1, xl, rows]

    def along(self, distance, xl):
        h = self.here
        if distance > 1:
            src = self.hop(distance - 1, xl, distance)
        else:
            src = self.slot(h.core, 0, xl)
        return self.copies.make(
            self.first + 2 * (distance - 1) + xl, src, self.hop(distance, xl), device(h.y, h.x, h.z + 1, h.core)
        )

    def over(self, distance):
        h = self.here
        return self.copies.make(
            self.first + 5 + distance,
            self.hop(distance, 1),
            self.slot(h.core, distance, 0),
            device(h.y + 1, h.x, h.z, h.core),
        )

    def beside(self, distance, xl, sending):
        h = self.here
        ref = self.slot(h.core if sending else 1 - h.core, distance, xl)
        return self.copies.make(
            self.first + 9 + 2 * distance + xl, ref, ref, device(h.y, h.x, h.z, 1 - h.core)
        )

    def begin(self, xl):
        self.copies.send(self.along(1, xl))
        self.copies.send(self.beside(0, xl, True))

    def place(self, distance, xl, source):
        at = self.rows(distance, (SPAN - 1 - distance) * self.count)
        self.kv[self.here.core, xl, at] = self.hops[distance - 1, source, self.rows(distance)]

    def arrival(self, distance, xl):
        wrapped = self.here.z < distance
        self.along(distance, xl).wait_recv()
        if distance < SPAN - 1:
            self.copies.send(self.along(distance + 1, xl))
        if xl == 1:
            self.copies.send(self.over(distance), wrapped)
            pl.when(jnp.logical_not(wrapped))(lambda: self.place(distance, 1, 1))
        else:
            pl.when(wrapped)(lambda: self.place(distance, 1, 0))
            pl.when(jnp.logical_not(wrapped))(lambda: self.place(distance, 0, 0))
            self.copies.send(self.beside(distance, 1, True))

    def placed(self, distance):
        pl.when(self.here.z < distance)(self.over(distance).wait_recv)
        self.copies.send(self.beside(distance, 0, True))

    def rest(self):
        for distance in range(SPAN):
            for xl in range(NX):
                self.beside(distance, xl, False).wait_recv()


class Products:
    def __init__(self, here, copies, own, other, part_a, part_b, whole_a, whole_b):
        self.here, self.copies, self.own, self.other = here, copies, own, other
        self.half_way = {1: part_a, -1: part_b}
        self.whole = {1: whole_a, -1: whole_b}
        self.first = copies.reserve(PRODUCT_COPIES)
        self.width = own.shape[-1] // 2

    def columns(self, half):
        return pl.ds(half * self.width, self.width)

    def beside(self, j, half):
        h = self.here
        return self.copies.make(
            self.first + 6 + 2 * j + half,
            self.own.at[1 - h.core, j, :, self.columns(half)],
            self.other.at[j, :, self.columns(half)],
            device(h.y, h.x, h.z, 1 - h.core),
        )

    def far(self, direction):
        h = self.here
        half = 0 if direction > 0 else 1
        return self.copies.make(
            self.first + half,
            self.own.at[h.core, 0, :, self.columns(half)],
            self.half_way[direction],
            device(h.y, h.x + direction, h.z, h.core),
        )

    def near(self, direction, half):
        h = self.here
        j = 1 if direction > 0 else 2
        return self.copies.make(
            self.first + 2 * j + half,
            self.own.at[h.core, j, :, self.columns(half)],
            self.whole[direction].at[:, self.columns(half)],
            device(h.y, h.x + direction, h.z, h.core),
        )

    def add(self, j, half, more=None):
        h = self.here
        tile = 512

        def body(step, _):
            inner = pl.multiple_of(step * tile, tile)
            at = pl.ds(pl.multiple_of(half * self.width + inner, tile), tile)
            total = self.own[h.core, j, :, at].astype(jnp.float32) + self.other[j, :, at].astype(jnp.float32)
            if more is not None:
                total = total + more[:, pl.ds(inner, tile)].astype(jnp.float32)
            self.own[h.core, j, :, at] = total.astype(jnp.bfloat16)
            return 0

        lax.fori_loop(0, self.width // tile, body, 0)

    def reduce(self, j):
        order = (1, 0) if j == 1 else (0, 1)
        for turn, half in enumerate(order):
            self.beside(j, half).wait_recv()
            if j == 0:
                self.add(0, half)
                self.copies.send(self.far(1 if half == 0 else -1))
            elif j < 3 and turn == 0:
                self.add(j, half)
                self.copies.send(self.near(1 if j == 1 else -1, half))

    def last(self, out):
        h = self.here
        for direction in (1, -1):
            j, half = (1, 0) if direction > 0 else (2, 1)
            self.far(direction).wait_recv()
            self.add(j, half, self.half_way[direction])
            self.copies.send(self.near(direction, half))
        for half in (0, 1):
            for direction in (1, -1):
                self.near(direction, half).wait_recv()
        tile = 512

        def body(step, _):
            at = pl.ds(pl.multiple_of(step * tile, tile), tile)
            total = self.own[h.core, 3, :, at].astype(jnp.float32) + self.other[3, :, at].astype(jnp.float32)
            for direction in (1, -1):
                total = total + self.whole[direction][:, at].astype(jnp.float32)
            out[:, at] = total.astype(out.dtype)
            return 0

        lax.fori_loop(0, 2 * self.width // tile, body, 0)


def neighbours(h):
    outer = h.x - 1 + 2 * h.xl
    return [
        device(h.y, h.x, h.z, 1 - h.core),
        device(h.y, h.xh * 2 + 1 - h.xl, h.z, h.core),
        device(h.y, h.xh * 2 + 1 - h.xl, h.z, 1 - h.core),
        device(h.y, outer, h.z, h.core),
        device(h.y + 1, h.x, h.z, h.core),
        device(h.y - 1, h.x, h.z, h.core),
        device(h.y, h.x, h.z + 1, h.core),
        device(h.y, h.x, h.z - 1, h.core),
    ]


def block_kernel(
    docs, tokens, gain, wq, wk, wv, wo, inner_cos, inner_sin, outer_cos, outer_sin, out,
    rows, qa, qb, qb_own, oa, ob, queries, kv, values, hops, attended,
    own, other, part_a, part_b, whole_a, whole_b, cosine, sine, bias, send_sems, recv_sems,
):
    h = Place()
    half_heads = wq.shape[1] // 2
    barrier = pltpu.get_barrier_semaphore()
    greeted = neighbours(h)
    for to in greeted:
        pl.semaphore_signal(barrier, inc=1, device_id=to, device_id_type=MESH)

    for p, kind in ((0, wk), (1, wv)):
        qb_own[p, :, :HD] = wq[:, p * half_heads + Q_A : (p + 1) * half_heads]
        qb_own[p, :, HD:] = kind[...]

    copies = Copies(send_sems, recv_sems)
    gathers = [Gather(h, copies, buf, z_first) for buf, z_first in ((qa, True), (qb, False), (oa, True), (ob, False))]
    token_rows = Tokens(h, copies, rows)
    relay = Relay(h, copies, kv, hops)
    products = Products(h, copies, own, other, part_a, part_b, whole_a, whole_b)

    pl.semaphore_wait(barrier, len(greeted))
    gathers[0].exchange([wq.at[:, pl.ds(p * half_heads, Q_A)] for p in (0, 1)])
    gathers[1].exchange([qb_own.at[p] for p in (0, 1)])

    def norm(step, _):
        at = pl.ds(pl.multiple_of(step * 32, 32), 32)
        value = tokens[at, :].astype(jnp.float32)
        scale = lax.rsqrt(jnp.mean(value * value, axis=-1, keepdims=True) + 1e-05)
        rows[h.xl, h.xh * 2 + h.core, at, :] = (value * scale * gain[...]).astype(jnp.bfloat16)
        return 0

    lax.fori_loop(0, BLOCK // 32, norm, 0)
    token_rows.begin()

    plans = [part.stages() for part in gathers]
    lengths = [len(plan) for plan in plans]

    def run(which, stage):
        for index in which:
            if 0 <= stage < lengths[index]:
                for step in plans[index][stage]:
                    step()

    def fill_tables():
        for xl in range(NX):
            context = (h.y * NX + xl) * NZ + h.z
            oc, os_ = outer_cos[context], outer_sin[context]
            cosine[xl] = inner_cos[...] * oc - inner_sin[...] * os_
            turned = inner_sin[...] * oc + inner_cos[...] * os_
            lane = lax.broadcasted_iota(jnp.int32, turned.shape, 1)
            sine[xl] = jnp.where(lane < HD // 2, -turned, turned)

        def mask(index, _):
            block = ((h.y * NX + index // NTP) * NZ + h.z) * NTP + lax.rem(index, NTP)
            for w in range(WINDOW):
                key = block - (WINDOW - 1) + w
                same = docs[lax.rem(key + docs.shape[0], docs.shape[0])] == docs[block]
                visible = jnp.logical_and(same, key >= 0)
                bias[index, :, w * BLOCK : (w + 1) * BLOCK] = jnp.full(
                    (1, BLOCK), jnp.where(visible, 0.0, neg_large), jnp.float32
                )
            return 0

        lax.fori_loop(0, NX * NTP, mask, 0)
        values[:, :, HD:] = jnp.ones_like(values[:, :, HD:])

    lag = 3
    for stage in range(max(lengths[:2])):
        run((0, 1), stage)
        if stage == 0:
            gathers[2].exchange([wo.at[:, pl.ds(p * half_heads, O_A)] for p in (0, 1)])
            gathers[3].exchange([wo.at[:, pl.ds(p * half_heads + O_A, half_heads - O_A)] for p in (0, 1)])
            fill_tables()
        if stage == 2:
            token_rows.first_hop(0)
        if stage == 5:
            token_rows.first_hop(1)
        run((2, 3), stage - lag)
    stage = max(lengths[:2]) - lag
    gathers[0].rest()
    gathers[1].rest()
    token_rows.second_hop()
    token_rows.rest()

    def project(weights, chip):
        at = pl.ds((chip // 2) * 2, 2)
        total = None
        depth = NX * NZ * weights.shape[3]
        for y in range(NY):
            left = rows[lax.rem(chip, 2), at, :, y * depth : (y + 1) * depth].reshape(2 * BLOCK, depth)
            term = jnp.dot(left, weights[y].reshape(depth, weights.shape[4]), preferred_element_type=jnp.float32)
            total = term if total is None else total + term
        return total

    def rotated(value, chip):
        at = pl.ds(pl.multiple_of((chip // 2) * (2 * BLOCK), 2 * BLOCK), 2 * BLOCK)
        swapped = pltpu.roll(value, HD // 2, 1)
        return value * cosine[lax.rem(chip, 2), at, :] + swapped * sine[lax.rem(chip, 2), at, :]

    def keep_query(value, chip, head):
        query = (rotated(value, chip) * HD ** (-0.5)).astype(jnp.bfloat16)
        for core in (0, 1):
            queries[lax.rem(chip, 2), (chip // 2) * 2 + core, head * BLOCK : (head + 1) * BLOCK, :] = query[
                core * BLOCK : (core + 1) * BLOCK
            ]

    def project_b(chip, _):
        total = project(qb, chip)
        keep_query(total[:, :HD], chip, 3)
        value = total[:, HD:]
        value = jnp.where(h.core == 0, rotated(value, chip), value).astype(jnp.bfloat16)
        start = (SPAN - 1) * NTP * BLOCK + (chip // 2) * (2 * BLOCK)
        kv[h.core, lax.rem(chip, 2), pl.ds(pl.multiple_of(start, 2 * BLOCK), 2 * BLOCK), :] = value
        return 0

    def project_a(chip, _):
        total = project(qa, chip)
        for head in range(3):
            keep_query(total[:, head * HD : (head + 1) * HD], chip, head)
        return 0

    for xl in (1, 0):
        lax.fori_loop(0, RING_X // NX, lambda xh, _: project_b(xh * 2 + xl, 0), 0)
        relay.begin(xl)
    run((2, 3), stage)
    lax.fori_loop(0, RING_X // 2, project_a, 0)
    run((2, 3), stage + 1)
    lax.fori_loop(RING_X // 2, RING_X, project_a, 0)
    stage += 2
    for distance in range(1, SPAN):
        for xl in (1, 0):
            relay.arrival(distance, xl)
        if distance > 1:
            relay.placed(distance - 1)
        run((2, 3), stage)
        stage += 1
    relay.placed(SPAN - 1)
    for stage in range(stage, max(lengths[2:])):
        run((2, 3), stage)
    relay.rest()
    gathers[2].rest()
    gathers[3].rest()

    for xl in range(NX):
        values[xl, :, :HD] = kv[1, xl]

    heads = half_heads // HD
    query_at = lax.broadcasted_iota(jnp.int32, (2 * BLOCK, BLOCK), 0)
    query_at = lax.rem(query_at, BLOCK)
    causal = jnp.where(query_at >= lax.broadcasted_iota(jnp.int32, (2 * BLOCK, BLOCK), 1), 0.0, neg_large)

    def attend(chip):
        xl, first_block = lax.rem(chip, 2), (chip // 2) * 2

        def body(step, _):
            block = first_block + step
            window = pl.ds(pl.multiple_of((block + SPAN * NTP - WINDOW - (NTP - 1)) * BLOCK, BLOCK), WINDOW * BLOCK)
            for pair in range(heads // 2):
                query = queries[xl, block, pair * 2 * BLOCK : (pair + 1) * 2 * BLOCK, :]
                scores = lax.dot_general(query, kv[0, xl, window, :], NT, preferred_element_type=jnp.float32)
                scores = scores + bias[xl * NTP + block]
                near = (WINDOW - 1) * BLOCK
                scores = jnp.concatenate([scores[:, :near], scores[:, near:] + causal], axis=1)
                top = jnp.max(scores, axis=-1, keepdims=True)
                weights = jnp.exp(scores - top).astype(jnp.bfloat16)
                total = jnp.dot(weights, values[xl, window, :], preferred_element_type=jnp.float32)
                result = (total[:, :HD] / total[:, HD:]).astype(jnp.bfloat16)
                for k in range(2):
                    head = pair * 2 + k
                    attended[xl, block, :, head * HD : (head + 1) * HD] = result[k * BLOCK : (k + 1) * BLOCK]
            return 0

        lax.fori_loop(0, 2, body, 0)

    def multiply(j, chip, half):
        xl, first_block = lax.rem(chip, 2), (chip // 2) * 2
        tile = NZ * wo.shape[0]

        def body(step, _):
            left = attended[xl, pl.ds(first_block, 2)].reshape(2 * BLOCK, half_heads)
            y, x = step // NX, lax.rem(step, NX)
            right = jnp.concatenate(
                [oa[y, x].reshape(tile, O_A), ob[y, x].reshape(tile, half_heads - O_A)], axis=1
            )
            total = lax.dot_general(left, right, NT, preferred_element_type=jnp.float32).astype(jnp.bfloat16)
            at = pl.ds(pl.multiple_of(step * tile, tile), tile)
            for core in (0, 1):
                own[core, j, :, at] = total[core * BLOCK : (core + 1) * BLOCK]
            return 0

        lax.fori_loop(half * (NY * NX // 2), (half + 1) * (NY * NX // 2), body, 0)

    for j, offset in enumerate((2, 1, 3, 0)):
        chip = lax.rem(h.x + offset, RING_X)
        attend(chip)
        if j > 1:
            products.reduce(j - 1)
        for half in (0, 1):
            multiply(j, chip, half)
            copies.send(products.beside(j, half))
        if j == 0:
            products.reduce(0)
    products.reduce(3)
    products.last(out)
    copies.finish()


COPIES = 2 * (COPIES_A + COPIES_B + 4) + 13 + RELAY_COPIES + PRODUCT_COPIES


def rotation_tables(count):
    half_width = HD // 2
    frequency = np.float32(rope_base) ** (-np.arange(half_width, dtype=np.float32) / np.float32(half_width))
    frequency = np.concatenate([frequency, frequency]).astype(np.float64)
    inner = np.arange(count)[:, None] * frequency
    outer = (np.arange(NY * NX * NZ) * count)[:, None, None] * frequency
    return [f(angle).astype(np.float32) for angle in (inner, outer) for f in (np.cos, np.sin)]


def whole_block(doc_blocks, tokens, gain, w_query, w_key, w_value, w_out_t):
    count, width = tokens.shape
    rows = w_query.shape[0]
    half = w_query.shape[1] // 2
    near = NTP * count
    bf16 = jnp.bfloat16
    vmem = pl.BlockSpec(memory_space=pltpu.VMEM)
    turns = rotation_tables(near)
    return pl.pallas_call(
        block_kernel,
        out_shape=jax.ShapeDtypeStruct((count, width), bf16),
        in_specs=[pl.BlockSpec(memory_space=pltpu.SMEM)] + [vmem] * 10,
        out_specs=vmem,
        scratch_shapes=[
            pltpu.VMEM((NX, NTP, count, width), bf16),
            pltpu.VMEM((NY, NX, NZ, rows, Q_A), bf16),
            pltpu.VMEM((NY, NX, NZ, rows, half - Q_A + HD), bf16),
            pltpu.VMEM((2, rows, half - Q_A + HD), bf16),
            pltpu.VMEM((NY, NX, NZ, rows, O_A), bf16),
            pltpu.VMEM((NY, NX, NZ, rows, half - O_A), bf16),
            pltpu.VMEM((NX, NTP, half // HD * BLOCK, HD), bf16),
            pltpu.VMEM((2, NX, SPAN * near, HD), bf16),
            pltpu.VMEM((NX, SPAN * near, 2 * HD), bf16),
            pltpu.VMEM((SPAN - 1, NX, near, HD), bf16),
            pltpu.VMEM((NX, NTP, count, half), bf16),
            pltpu.VMEM((2, RING_X, count, width), bf16),
            pltpu.VMEM((RING_X, count, width), bf16),
            pltpu.VMEM((count, width // 2), bf16),
            pltpu.VMEM((count, width // 2), bf16),
            pltpu.VMEM((count, width), bf16),
            pltpu.VMEM((count, width), bf16),
            pltpu.VMEM((NX, near, HD), jnp.float32),
            pltpu.VMEM((NX, near, HD), jnp.float32),
            pltpu.VMEM((NX * NTP, 1, WINDOW * BLOCK), jnp.float32),
            pltpu.SemaphoreType.DMA((COPIES,)),
            pltpu.SemaphoreType.DMA((COPIES,)),
        ],
        compiler_params=pltpu.CompilerParams(
            collective_id=0, has_side_effects=True, vmem_limit_bytes=60 * 1024 * 1024
        ),
    )(doc_blocks, tokens, gain, w_query, w_key, w_value, w_out_t, *turns)


def local(tokens, norm_gain, w_query, w_key, w_value, w_out, doc_blocks):
    return whole_block(doc_blocks, tokens, norm_gain[None, :], w_query, w_key, w_value, w_out.T)


def solution(mesh):
    return jax.shard_map(
        local,
        mesh=mesh,
        in_specs=(
            P(("ctx", "tp"), None),
            P(),
            P("ctx", "tp"),
            P("ctx", "tp"),
            P("ctx", "tp"),
            P("tp", "ctx"),
            P(),
        ),
        out_specs=P(("ctx", "tp"), None),
        check_vma=False,
    )
```

```python
import functools

import jax
import jax.numpy as jnp
import numpy as np
from jax import lax
from jax.experimental import pallas as pl
from jax.experimental.pallas import tpu as pltpu
from jax.sharding import PartitionSpec as P

HD = 128
BLOCK = 128
WINDOW = 12
SPAN = 4
NY, NX, NZ, NTP = 4, 2, 8, 4
RING_X = 4
MESH = pl.DeviceIdType.MESH

rope_base = 500000.0
neg_large = -1e30

Z_OFFSETS = [0, -1, 1, -2, 2, -3, 3, 4]
Y_OFFSETS = [0, -1, 1, 2]
TILE_OFFSETS = [0, 1, -1, 2]
COPIES_A = 8 + 32
COPIES_B = 4 + 32
RELAY_COPIES = 17
PRODUCT_COPIES = 14 * NY
Q_A = 384
NT = (((1,), (1,)), ((), ()))


class Place:
    def __init__(self):
        c, t = lax.axis_index("ctx"), lax.axis_index("tp")
        self.y, self.xl, self.z = c // (NX * NZ), lax.rem(c // NZ, NX), lax.rem(c, NZ)
        self.xh, self.core = t // 2, lax.rem(t, 2)
        self.x = self.xh * 2 + self.xl


def device(y, x, z, core):
    x = lax.rem(x + RING_X, RING_X)
    ctx = (lax.rem(y + NY, NY) * NX + lax.rem(x, 2)) * NZ + lax.rem(z + NZ, NZ)
    return (ctx, (x // 2) * 2 + core)


class Copies:
    def __init__(self, send_sems, recv_sems):
        self.send_sems, self.recv_sems = send_sems, recv_sems
        self.used = 0
        self.sent = []

    def reserve(self, count):
        first = self.used
        self.used += count
        return first

    def make(self, index, src, dst, to, recv_index=None):
        return pltpu.make_async_remote_copy(
            src_ref=src,
            dst_ref=dst,
            send_sem=self.send_sems.at[index],
            recv_sem=self.recv_sems.at[index if recv_index is None else recv_index],
            device_id=to,
            device_id_type=MESH,
        )

    def send(self, copy, when=None):
        if when is None:
            copy.start()
        else:
            pl.when(when)(copy.start)
        self.sent.append((copy, when))

    def finish(self):
        for copy, when in self.sent:
            if when is None:
                copy.wait_send()
            else:
                pl.when(when)(copy.wait_send)


class Gather:
    def __init__(self, here, copies, buf, z_first):
        self.here, self.copies, self.buf, self.z_first = here, copies, buf, z_first
        self.first = copies.reserve(COPIES_A if z_first else COPIES_B)
        self.arrive = copies.reserve(2)

    def exchange(self, parts):
        h = self.here
        for p in (0, 1):
            local = jnp.logical_and(h.core == h.xl, h.core == p)

            @pl.when(local)
            def _():
                self.buf[h.y, h.xl, h.z] = parts[p][...]

            copy = self.copies.make(
                self.arrive + p,
                parts[p],
                self.buf.at[h.y, h.xl, h.z],
                device(h.y, h.xh * 2 + h.core, h.z, p),
                self.arrive + h.xl,
            )
            self.copies.send(copy, jnp.logical_not(local))

    def exchanged(self):
        h = self.here
        for slot in (0, 1):
            local = jnp.logical_and(h.core == h.xl, h.xl == slot)
            ref = self.buf.at[h.y, slot, h.z]
            copy = self.copies.make(self.arrive + slot, ref, ref, device(h.y, h.x + 1, h.z, h.core))
            pl.when(jnp.logical_not(local))(copy.wait_recv)

    def copy(self, index, yy, zz, half, to):
        yy, zz = lax.rem(yy + 2 * NY, NY), lax.rem(zz + 2 * NZ, NZ)
        ref = self.buf.at[yy, :, zz] if half is None else self.buf.at[yy, half, zz]
        return self.copies.make(self.first + index, ref, ref, to)

    def ring_id(self, second, block, direction, hop, length):
        base = 0 if not second else (NZ if self.z_first else NY) + block * length
        return base + (0 if direction > 0 else length // 2) + hop - 1

    def along_z(self, second, y_offset, block, direction, hop, sending):
        h = self.here
        distance = hop - 1 if sending else hop
        half = (0 if direction > 0 else 1) if hop == NZ // 2 else None
        return self.copy(
            self.ring_id(second, block, direction, hop, NZ),
            h.y + y_offset,
            h.z - direction * distance,
            half,
            device(h.y, h.x, h.z + direction, h.core),
        )

    def along_y(self, second, z_offset, block, direction, hop, sending):
        h = self.here
        distance = hop - 1 if sending else hop
        half = (0 if direction > 0 else 1) if hop == NY // 2 else None
        return self.copy(
            self.ring_id(second, block, direction, hop, NY),
            h.y - direction * distance,
            h.z + z_offset,
            half,
            device(h.y + direction, h.x, h.z, h.core),
        )

    def first_ring(self, direction, hop, sending):
        along = self.along_z if self.z_first else self.along_y
        return along(False, 0, 0, direction, hop, sending)

    def second_ring(self, block, direction, hop, sending):
        if self.z_first:
            return self.along_y(True, Z_OFFSETS[block], block, direction, hop, sending)
        return self.along_z(True, Y_OFFSETS[block], block, direction, hop, sending)

    def begin(self):
        self.exchanged()
        for direction in (1, -1):
            self.copies.send(self.first_ring(direction, 1, True))
        for direction in (1, -1):
            self.copies.send(self.second_ring(0, direction, 1, True))

    def first_arrival(self, hop):
        half_way = (NZ if self.z_first else NY) // 2
        for turn, direction in enumerate((1, -1)):
            self.first_ring(direction, hop, False).wait_recv()
            if hop < half_way:
                self.copies.send(self.first_ring(direction, hop + 1, True))
                for across in (1, -1):
                    self.copies.send(self.second_ring(2 * hop - 1 + turn, across, 1, True))
        if hop == half_way:
            for across in (1, -1):
                self.copies.send(self.second_ring(2 * hop - 1, across, 1, True))

    def second_arrival(self, block, hop):
        half_way = (NY if self.z_first else NZ) // 2
        for direction in (1, -1):
            self.second_ring(block, direction, hop, False).wait_recv()
            if hop < half_way:
                self.copies.send(self.second_ring(block, direction, hop + 1, True))

    def stages(self):
        blocks, ring, across = (NZ, NZ, NY) if self.z_first else (NY, NY, NZ)
        out = [[self.begin]]
        for hop in range(1, ring // 2 + 1):
            out.append([functools.partial(self.first_arrival, hop)])
        for b in range(blocks):
            for hop in range(1, across // 2):
                at = (b + 1) // 2 + hop
                while len(out) <= at:
                    out.append([])
                out[at].append(functools.partial(self.second_arrival, b, hop))
        return out

    def rest(self):
        blocks, across = (NZ, NY) if self.z_first else (NY, NZ)
        for b in range(blocks):
            self.second_arrival(b, across // 2)


class Columns(Gather):
    def __init__(self, here, copies, buf):
        super().__init__(here, copies, buf, True)

    def across(self, block, direction, hop, sending):
        h = self.here
        return self.copy(
            self.ring_id(True, block, direction, hop, NY),
            h.y - direction * (hop - 1 if sending else hop),
            h.z + Z_OFFSETS[block],
            None,
            device(h.y + direction, h.x, h.z, h.core),
        )

    def ring_begin(self):
        self.exchanged()
        for direction in (1, -1):
            self.copies.send(self.first_ring(direction, 1, True))

    def ring_arrival(self, hop):
        for direction in (1, -1):
            self.first_ring(direction, hop, False).wait_recv()
            if hop < NZ // 2:
                self.copies.send(self.first_ring(direction, hop + 1, True))

    def send_across(self, direction, blocks=range(NZ)):
        for block in blocks:
            self.copies.send(self.across(block, direction, 1, True))

    def pass_across(self, blocks):
        for block in blocks:
            self.across(block, -1, 1, False).wait_recv()
            self.copies.send(self.across(block, -1, 2, True))

    def await_tile(self, tile):
        if tile >= 2:
            for block in range(NZ):
                self.across(block, 1 if tile == 2 else -1, tile - 1 if tile == 2 else 2, False).wait_recv()


class Tokens:
    def __init__(self, here, copies, rows):
        self.here, self.copies, self.rows = here, copies, rows
        self.first = copies.reserve(13)

    def part(self, x, core, half):
        x = lax.rem(x + RING_X, RING_X)
        ref = self.rows.at[lax.rem(x, 2), (x // 2) * 2 + core]
        return ref if half is None else ref.at[pl.ds(half * (BLOCK // 2), BLOCK // 2)]

    def ring(self, direction, hop, half, sending):
        h = self.here
        index = (0 if direction > 0 else 2) + half if hop == 1 else 4 + half
        ref = self.part(h.x - direction * (hop - 1 if sending else hop), h.core, half)
        return self.copies.make(self.first + index, ref, ref, device(h.y, h.x + direction, h.z, h.core))

    def beside(self, distance, half, sending):
        h = self.here
        index = 6 if half is None else {-1: 7, 1: 9, 2: 11}[distance] + half
        ref = self.part(h.x + distance, h.core if sending else 1 - h.core, half)
        return self.copies.make(self.first + index, ref, ref, device(h.y, h.x, h.z, 1 - h.core))

    def begin(self):
        for turn in (0, 1):
            self.copies.send(self.ring(1, 1, turn, True))
            self.copies.send(self.ring(-1, 1, 1 - turn, True))
        self.copies.send(self.beside(0, None, True))

    def first_hop(self, turn):
        for direction in (1, -1):
            half = turn if direction > 0 else 1 - turn
            self.ring(direction, 1, half, False).wait_recv()
            if turn == 0:
                self.copies.send(self.ring(direction, 2, half, True))
            self.copies.send(self.beside(-direction, half, True))

    def second_hop(self):
        for direction, half in ((1, 0), (-1, 1)):
            self.ring(direction, 2, half, False).wait_recv()
            self.copies.send(self.beside(2, half, True))

    def rest(self):
        self.beside(0, None, False).wait_recv()
        for distance in (-1, 1, 2):
            for half in (0, 1):
                self.beside(distance, half, False).wait_recv()


class Relay:
    def __init__(self, here, copies, kv, hops):
        self.here, self.copies, self.kv, self.hops = here, copies, kv, hops
        self.first = copies.reserve(RELAY_COPIES)
        self.count = kv.shape[2] // SPAN

    def rows(self, distance, offset=0):
        skipped = BLOCK if distance == SPAN - 1 else 0
        return pl.ds(offset + skipped, self.count - skipped)

    def slot(self, kind, distance, xl):
        return self.kv.at[kind, xl, self.rows(distance, (SPAN - 1 - distance) * self.count)]

    def hop(self, distance, xl, needed=None):
        rows = self.rows(distance if needed is None else needed)
        return self.hops.at[distance - 1, xl, rows]

    def along(self, distance, xl):
        h = self.here
        if distance > 1:
            src = self.hop(distance - 1, xl, distance)
        else:
            src = self.slot(h.core, 0, xl)
        return self.copies.make(
            self.first + 2 * (distance - 1) + xl, src, self.hop(distance, xl), device(h.y, h.x, h.z + 1, h.core)
        )

    def over(self, distance):
        h = self.here
        return self.copies.make(
            self.first + 5 + distance,
            self.hop(distance, 1),
            self.slot(h.core, distance, 0),
            device(h.y + 1, h.x, h.z, h.core),
        )

    def beside(self, distance, xl, sending):
        h = self.here
        ref = self.slot(h.core if sending else 1 - h.core, distance, xl)
        return self.copies.make(
            self.first + 9 + 2 * distance + xl, ref, ref, device(h.y, h.x, h.z, 1 - h.core)
        )

    def begin(self, xl):
        self.copies.send(self.along(1, xl))
        self.copies.send(self.beside(0, xl, True))

    def place(self, distance, xl, source):
        at = self.rows(distance, (SPAN - 1 - distance) * self.count)
        self.kv[self.here.core, xl, at] = self.hops[distance - 1, source, self.rows(distance)]

    def arrival(self, distance, xl):
        wrapped = self.here.z < distance
        self.along(distance, xl).wait_recv()
        if distance < SPAN - 1:
            self.copies.send(self.along(distance + 1, xl))
        if xl == 1:
            self.copies.send(self.over(distance), wrapped)
            pl.when(jnp.logical_not(wrapped))(lambda: self.place(distance, 1, 1))
        else:
            pl.when(wrapped)(lambda: self.place(distance, 1, 0))
            pl.when(jnp.logical_not(wrapped))(lambda: self.place(distance, 0, 0))
            self.copies.send(self.beside(distance, 1, True))

    def placed(self, distance):
        pl.when(self.here.z < distance)(self.over(distance).wait_recv)
        self.copies.send(self.beside(distance, 0, True))

    def rest(self):
        for distance in range(SPAN):
            for xl in range(NX):
                self.beside(distance, xl, False).wait_recv()


class Products:
    def __init__(self, here, copies, own, other, part_a, part_b, whole_a, whole_b):
        self.here, self.copies, self.own, self.other = here, copies, own, other
        self.half_way = {1: part_a, -1: part_b}
        self.whole = {1: whole_a, -1: whole_b}
        self.first = copies.reserve(PRODUCT_COPIES)
        self.width = own.shape[-1]

    def columns(self, tile, half):
        y = lax.rem(self.here.y + TILE_OFFSETS[tile] + NY, NY)
        return pl.ds(pl.multiple_of((2 * y + half) * self.width, self.width), self.width)

    def beside(self, tile, j, half):
        h = self.here
        return self.copies.make(
            self.first + 14 * tile + 6 + 2 * j + half,
            self.own.at[1 - h.core, j, 2 * tile + half],
            self.other.at[j, 2 * tile + half],
            device(h.y, h.x, h.z, 1 - h.core),
        )

    def far_place(self, tile, direction):
        return self.half_way[direction].at[tile]

    def far(self, tile, direction):
        h = self.here
        half = 0 if direction > 0 else 1
        return self.copies.make(
            self.first + 14 * tile + half,
            self.own.at[h.core, 0, 2 * tile + half],
            self.far_place(tile, direction),
            device(h.y, h.x + direction, h.z, h.core),
        )

    def near(self, tile, direction, half):
        h = self.here
        j = 1 if direction > 0 else 2
        return self.copies.make(
            self.first + 14 * tile + 2 * j + half,
            self.own.at[h.core, j, 2 * tile + half],
            self.whole[direction].at[2 * tile + half],
            device(h.y, h.x + direction, h.z, h.core),
        )

    def add(self, tile, j, half, more=None):
        h = self.here
        at = 2 * tile + half
        total = self.own[h.core, j, at].astype(jnp.float32) + self.other[j, at].astype(jnp.float32)
        if more is not None:
            total = total + more[...].astype(jnp.float32)
        self.own[h.core, j, at] = total.astype(jnp.bfloat16)

    def reduce(self, tile, j):
        order = (1, 0) if j == 1 else (0, 1)
        for turn, half in enumerate(order):
            self.beside(tile, j, half).wait_recv()
            if j == 0:
                self.add(tile, 0, half)
                self.copies.send(self.far(tile, 1 if half == 0 else -1))
            elif j < 3 and turn == 0:
                self.add(tile, j, half)
                self.copies.send(self.near(tile, 1 if j == 1 else -1, half))

    def pass_on(self, tile):
        for direction in (1, -1):
            j, half = (1, 0) if direction > 0 else (2, 1)
            self.far(tile, direction).wait_recv()
            self.add(tile, j, half, self.far_place(tile, direction))
            self.copies.send(self.near(tile, direction, half))

    def last(self, tile, out):
        h = self.here
        for half in (0, 1):
            for direction in (1, -1):
                self.near(tile, direction, half).wait_recv()
        for half in (0, 1):
            at = 2 * tile + half
            total = self.own[h.core, 3, at].astype(jnp.float32) + self.other[3, at].astype(jnp.float32)
            for direction in (1, -1):
                total = total + self.whole[direction][at].astype(jnp.float32)
            out[:, self.columns(tile, half)] = total.astype(out.dtype)


def neighbours(h):
    outer = h.x - 1 + 2 * h.xl
    return [
        device(h.y, h.x, h.z, 1 - h.core),
        device(h.y, h.xh * 2 + 1 - h.xl, h.z, h.core),
        device(h.y, h.xh * 2 + 1 - h.xl, h.z, 1 - h.core),
        device(h.y, outer, h.z, h.core),
        device(h.y + 1, h.x, h.z, h.core),
        device(h.y - 1, h.x, h.z, h.core),
        device(h.y, h.x, h.z + 1, h.core),
        device(h.y, h.x, h.z - 1, h.core),
    ]


def block_kernel(
    docs, tokens, gain, wq, wk, wv, wo, inner_cos, inner_sin, outer_cos, outer_sin, out,
    rows, qa, qb, qb_own, oa, queries, kv, values, hops, attended,
    own, other, part_a, part_b, whole_a, whole_b, cosine, sine, bias, send_sems, recv_sems,
):
    h = Place()
    half_heads = wq.shape[1] // 2
    barrier = pltpu.get_barrier_semaphore()
    greeted = neighbours(h)
    for to in greeted:
        pl.semaphore_signal(barrier, inc=1, device_id=to, device_id_type=MESH)

    for p, kind in ((0, wk), (1, wv)):
        qb_own[p, :, :HD] = wq[:, p * half_heads + Q_A : (p + 1) * half_heads]
        qb_own[p, :, HD:] = kind[...]

    copies = Copies(send_sems, recv_sems)
    gathers = [Gather(h, copies, buf, z_first) for buf, z_first in ((qa, True), (qb, False))]
    columns = Columns(h, copies, oa)
    token_rows = Tokens(h, copies, rows)
    relay = Relay(h, copies, kv, hops)
    products = Products(h, copies, own, other, part_a, part_b, whole_a, whole_b)

    pl.semaphore_wait(barrier, len(greeted))
    gathers[0].exchange([wq.at[:, pl.ds(p * half_heads, Q_A)] for p in (0, 1)])
    gathers[1].exchange([qb_own.at[p] for p in (0, 1)])
    columns.exchange([wo.at[:, pl.ds(p * half_heads, half_heads)] for p in (0, 1)])

    def norm(step, _):
        at = pl.ds(pl.multiple_of(step * 32, 32), 32)
        value = tokens[at, :].astype(jnp.float32)
        scale = lax.rsqrt(jnp.mean(value * value, axis=-1, keepdims=True) + 1e-05)
        rows[h.xl, h.xh * 2 + h.core, at, :] = (value * scale * gain[...]).astype(jnp.bfloat16)
        return 0

    lax.fori_loop(0, BLOCK // 32, norm, 0)
    token_rows.begin()

    plans = [part.stages() for part in gathers]

    def run(stage):
        for plan in plans:
            if stage < len(plan):
                for step in plan[stage]:
                    step()

    def fill_tables():
        for xl in range(NX):
            context = (h.y * NX + xl) * NZ + h.z
            oc, os_ = outer_cos[context], outer_sin[context]
            cosine[xl] = inner_cos[...] * oc - inner_sin[...] * os_
            turned = inner_sin[...] * oc + inner_cos[...] * os_
            lane = lax.broadcasted_iota(jnp.int32, turned.shape, 1)
            sine[xl] = jnp.where(lane < HD // 2, -turned, turned)

        def mask(index, _):
            block = ((h.y * NX + index // NTP) * NZ + h.z) * NTP + lax.rem(index, NTP)
            for w in range(WINDOW):
                key = block - (WINDOW - 1) + w
                same = docs[lax.rem(key + docs.shape[0], docs.shape[0])] == docs[block]
                visible = jnp.logical_and(same, key >= 0)
                bias[index, :, w * BLOCK : (w + 1) * BLOCK] = jnp.full(
                    (1, BLOCK), jnp.where(visible, 0.0, neg_large), jnp.float32
                )
            return 0

        lax.fori_loop(0, NX * NTP, mask, 0)
        values[:, :, HD:] = jnp.ones_like(values[:, :, HD:])

    for stage in range(max(len(plan) for plan in plans)):
        run(stage)
        if stage == 0:
            fill_tables()
        if stage == 2:
            token_rows.first_hop(0)
            columns.ring_begin()
        if stage == 4:
            columns.ring_arrival(1)
        if stage == 5:
            token_rows.first_hop(1)
            columns.ring_arrival(2)
    gathers[0].rest()
    gathers[1].rest()
    columns.send_across(-1, range(5))
    columns.ring_arrival(3)
    columns.send_across(-1, range(5, 7))
    token_rows.second_hop()
    token_rows.rest()

    def project(weights, chip):
        at = pl.ds((chip // 2) * 2, 2)
        total = None
        depth = NX * NZ * weights.shape[3]
        for y in range(NY):
            left = rows[lax.rem(chip, 2), at, :, y * depth : (y + 1) * depth].reshape(2 * BLOCK, depth)
            term = jnp.dot(left, weights[y].reshape(depth, weights.shape[4]), preferred_element_type=jnp.float32)
            total = term if total is None else total + term
        return total

    def rotated(value, chip):
        at = pl.ds(pl.multiple_of((chip // 2) * (2 * BLOCK), 2 * BLOCK), 2 * BLOCK)
        swapped = pltpu.roll(value, HD // 2, 1)
        return value * cosine[lax.rem(chip, 2), at, :] + swapped * sine[lax.rem(chip, 2), at, :]

    def keep_query(value, chip, head):
        query = (rotated(value, chip) * HD ** (-0.5)).astype(jnp.bfloat16)
        for core in (0, 1):
            queries[lax.rem(chip, 2), (chip // 2) * 2 + core, head * BLOCK : (head + 1) * BLOCK, :] = query[
                core * BLOCK : (core + 1) * BLOCK
            ]

    def project_b(chip, _):
        total = project(qb, chip)
        keep_query(total[:, :HD], chip, 3)
        value = total[:, HD:]
        value = jnp.where(h.core == 0, rotated(value, chip), value).astype(jnp.bfloat16)
        start = (SPAN - 1) * NTP * BLOCK + (chip // 2) * (2 * BLOCK)
        kv[h.core, lax.rem(chip, 2), pl.ds(pl.multiple_of(start, 2 * BLOCK), 2 * BLOCK), :] = value
        return 0

    def project_a(chip, _):
        total = project(qa, chip)
        for head in range(3):
            keep_query(total[:, head * HD : (head + 1) * HD], chip, head)
        return 0

    for xl in (1, 0):
        lax.fori_loop(0, RING_X // NX, lambda xh, _: project_b(xh * 2 + xl, 0), 0)
        relay.begin(xl)
    lax.fori_loop(0, RING_X, project_a, 0)
    columns.ring_arrival(4)
    columns.send_across(-1, range(7, NZ))
    for distance in range(1, SPAN):
        for xl in (1, 0):
            relay.arrival(distance, xl)
        if distance > 1:
            relay.placed(distance - 1)
        columns.pass_across(range(2 * distance - 2, 2 * distance))
    relay.placed(SPAN - 1)
    columns.send_across(1)
    relay.rest()

    for xl in range(NX):
        values[xl, :, :HD] = kv[1, xl]

    heads = half_heads // HD
    query_at = lax.broadcasted_iota(jnp.int32, (2 * BLOCK, BLOCK), 0)
    query_at = lax.rem(query_at, BLOCK)
    causal = jnp.where(query_at >= lax.broadcasted_iota(jnp.int32, (2 * BLOCK, BLOCK), 1), 0.0, neg_large)

    def attend(chip):
        xl, first_block = lax.rem(chip, 2), (chip // 2) * 2

        def body(step, _):
            block = first_block + step
            window = pl.ds(pl.multiple_of((block + SPAN * NTP - WINDOW - (NTP - 1)) * BLOCK, BLOCK), WINDOW * BLOCK)
            for pair in range(heads // 2):
                query = queries[xl, block, pair * 2 * BLOCK : (pair + 1) * 2 * BLOCK, :]
                scores = lax.dot_general(query, kv[0, xl, window, :], NT, preferred_element_type=jnp.float32)
                scores = scores + bias[xl * NTP + block]
                near = (WINDOW - 1) * BLOCK
                scores = jnp.concatenate([scores[:, :near], scores[:, near:] + causal], axis=1)
                top = jnp.max(scores, axis=-1, keepdims=True)
                weights = jnp.exp(scores - top).astype(jnp.bfloat16)
                total = jnp.dot(weights, values[xl, window, :], preferred_element_type=jnp.float32)
                result = (total[:, :HD] / total[:, HD:]).astype(jnp.bfloat16)
                for k in range(2):
                    head = pair * 2 + k
                    attended[xl, block, :, head * HD : (head + 1) * HD] = result[k * BLOCK : (k + 1) * BLOCK]
            return 0

        lax.fori_loop(0, 2, body, 0)

    order = (2, 1, 3, 0)

    def multiply(tile, j):
        chip = lax.rem(h.x + order[j], RING_X)
        left = attended[lax.rem(chip, 2), pl.ds((chip // 2) * 2, 2)].reshape(2 * BLOCK, half_heads)
        y = lax.rem(h.y + TILE_OFFSETS[tile] + NY, NY)
        depth = NZ * wo.shape[0]

        for half in (0, 1):
            right = oa[y, half].reshape(depth, half_heads)
            total = lax.dot_general(left, right, NT, preferred_element_type=jnp.float32).astype(jnp.bfloat16)
            for core in (0, 1):
                own[core, j, 2 * tile + half] = total[core * BLOCK : (core + 1) * BLOCK]
            copies.send(products.beside(tile, j, half))

    for j in range(RING_X):
        attend(lax.rem(h.x + order[j], RING_X))
        if j > 1:
            products.reduce(0, j - 1)
        multiply(0, j)
        if j == 0:
            products.reduce(0, 0)
    products.pass_on(0)
    columns.pass_across(range(6, NZ))
    for tile in range(1, NY):
        columns.await_tile(tile)
        for j in range(RING_X):
            multiply(tile, j)
        products.reduce(tile - 1, 3)
        products.reduce(tile, 0)
        if tile > 1:
            products.pass_on(tile - 1)
        products.reduce(tile, 1)
        products.reduce(tile, 2)
    products.pass_on(NY - 1)
    products.reduce(NY - 1, 3)
    for tile in range(NY):
        products.last(tile, out)
    copies.finish()


COPIES = 2 * COPIES_A + COPIES_B + 6 + 13 + RELAY_COPIES + PRODUCT_COPIES


def rotation_tables(count):
    half_width = HD // 2
    frequency = np.float32(rope_base) ** (-np.arange(half_width, dtype=np.float32) / np.float32(half_width))
    frequency = np.concatenate([frequency, frequency]).astype(np.float64)
    inner = np.arange(count)[:, None] * frequency
    outer = (np.arange(NY * NX * NZ) * count)[:, None, None] * frequency
    return [f(angle).astype(np.float32) for angle in (inner, outer) for f in (np.cos, np.sin)]


def whole_block(doc_blocks, tokens, gain, w_query, w_key, w_value, w_out_t):
    count, width = tokens.shape
    rows = w_query.shape[0]
    half = w_query.shape[1] // 2
    near = NTP * count
    bf16 = jnp.bfloat16
    vmem = pl.BlockSpec(memory_space=pltpu.VMEM)
    turns = rotation_tables(near)
    return pl.pallas_call(
        block_kernel,
        out_shape=jax.ShapeDtypeStruct((count, width), bf16),
        in_specs=[pl.BlockSpec(memory_space=pltpu.SMEM)] + [vmem] * 10,
        out_specs=vmem,
        scratch_shapes=[
            pltpu.VMEM((NX, NTP, count, width), bf16),
            pltpu.VMEM((NY, NX, NZ, rows, Q_A), bf16),
            pltpu.VMEM((NY, NX, NZ, rows, half - Q_A + HD), bf16),
            pltpu.VMEM((2, rows, half - Q_A + HD), bf16),
            pltpu.VMEM((NY, NX, NZ, rows, half), bf16),
            pltpu.VMEM((NX, NTP, half // HD * BLOCK, HD), bf16),
            pltpu.VMEM((2, NX, SPAN * near, HD), bf16),
            pltpu.VMEM((NX, SPAN * near, 2 * HD), bf16),
            pltpu.VMEM((SPAN - 1, NX, near, HD), bf16),
            pltpu.VMEM((NX, NTP, count, half), bf16),
            pltpu.VMEM((2, RING_X, 2 * NY, count, width // (2 * NY)), bf16),
            pltpu.VMEM((RING_X, 2 * NY, count, width // (2 * NY)), bf16),
            pltpu.VMEM((NY, count, width // (2 * NY)), bf16),
            pltpu.VMEM((NY, count, width // (2 * NY)), bf16),
            pltpu.VMEM((2 * NY, count, width // (2 * NY)), bf16),
            pltpu.VMEM((2 * NY, count, width // (2 * NY)), bf16),
            pltpu.VMEM((NX, near, HD), jnp.float32),
            pltpu.VMEM((NX, near, HD), jnp.float32),
            pltpu.VMEM((NX * NTP, 1, WINDOW * BLOCK), jnp.float32),
            pltpu.SemaphoreType.DMA((COPIES,)),
            pltpu.SemaphoreType.DMA((COPIES,)),
        ],
        compiler_params=pltpu.CompilerParams(
            collective_id=0, has_side_effects=True, vmem_limit_bytes=60 * 1024 * 1024
        ),
    )(doc_blocks, tokens, gain, w_query, w_key, w_value, w_out_t, *turns)


def local(tokens, norm_gain, w_query, w_key, w_value, w_out, doc_blocks):
    return whole_block(doc_blocks, tokens, norm_gain[None, :], w_query, w_key, w_value, w_out.T)


def solution(mesh):
    return jax.shard_map(
        local,
        mesh=mesh,
        in_specs=(
            P(("ctx", "tp"), None),
            P(),
            P("ctx", "tp"),
            P("ctx", "tp"),
            P("ctx", "tp"),
            P("tp", "ctx"),
            P(),
        ),
        out_specs=P(("ctx", "tp"), None),
        check_vma=False,
    )
```

```python
import functools

import jax
import jax.numpy as jnp
import numpy as np
from jax import lax
from jax.experimental import pallas as pl
from jax.experimental.pallas import tpu as pltpu
from jax.sharding import PartitionSpec as P

HD = 128
BLOCK = 128
WINDOW = 12
SPAN = 4
NY, NX, NZ, NTP = 4, 2, 8, 4
RING_X = 4
MESH = pl.DeviceIdType.MESH

rope_base = 500000.0
neg_large = -1e30

Z_OFFSETS = [0, -1, 1, -2, 2, -3, 3, 4]
Y_OFFSETS = [0, -1, 1, 2]
TILE_OFFSETS = [0, 1, -1, 2]
COPIES_A = 8 + 32
COPIES_B = 4 + 32
RELAY_COPIES = 17
PRODUCT_COPIES = 14 * NY
Q_A = 384
NT = (((1,), (1,)), ((), ()))


class Place:
    def __init__(self):
        c, t = lax.axis_index("ctx"), lax.axis_index("tp")
        self.y, self.xl, self.z = c // (NX * NZ), lax.rem(c // NZ, NX), lax.rem(c, NZ)
        self.xh, self.core = t // 2, lax.rem(t, 2)
        self.x = self.xh * 2 + self.xl


def device(y, x, z, core):
    x = lax.rem(x + RING_X, RING_X)
    ctx = (lax.rem(y + NY, NY) * NX + lax.rem(x, 2)) * NZ + lax.rem(z + NZ, NZ)
    return (ctx, (x // 2) * 2 + core)


class Copies:
    def __init__(self, send_sems, recv_sems):
        self.send_sems, self.recv_sems = send_sems, recv_sems
        self.used = 0
        self.sent = []

    def reserve(self, count):
        first = self.used
        self.used += count
        return first

    def make(self, index, src, dst, to, recv_index=None):
        return pltpu.make_async_remote_copy(
            src_ref=src,
            dst_ref=dst,
            send_sem=self.send_sems.at[index],
            recv_sem=self.recv_sems.at[index if recv_index is None else recv_index],
            device_id=to,
            device_id_type=MESH,
        )

    def send(self, copy, when=None):
        if when is None:
            copy.start()
        else:
            pl.when(when)(copy.start)
        self.sent.append((copy, when))

    def finish(self):
        for copy, when in self.sent:
            if when is None:
                copy.wait_send()
            else:
                pl.when(when)(copy.wait_send)


class Gather:
    def __init__(self, here, copies, buf, z_first):
        self.here, self.copies, self.buf, self.z_first = here, copies, buf, z_first
        self.first = copies.reserve(COPIES_A if z_first else COPIES_B)
        self.arrive = copies.reserve(2)

    def exchange(self, parts):
        h = self.here
        for p in (0, 1):
            local = jnp.logical_and(h.core == h.xl, h.core == p)

            @pl.when(local)
            def _():
                self.buf[h.y, h.xl, h.z] = parts[p][...]

            copy = self.copies.make(
                self.arrive + p,
                parts[p],
                self.buf.at[h.y, h.xl, h.z],
                device(h.y, h.xh * 2 + h.core, h.z, p),
                self.arrive + h.xl,
            )
            self.copies.send(copy, jnp.logical_not(local))

    def exchanged(self):
        h = self.here
        for slot in (0, 1):
            local = jnp.logical_and(h.core == h.xl, h.xl == slot)
            ref = self.buf.at[h.y, slot, h.z]
            copy = self.copies.make(self.arrive + slot, ref, ref, device(h.y, h.x + 1, h.z, h.core))
            pl.when(jnp.logical_not(local))(copy.wait_recv)

    def copy(self, index, yy, zz, half, to):
        yy, zz = lax.rem(yy + 2 * NY, NY), lax.rem(zz + 2 * NZ, NZ)
        ref = self.buf.at[yy, :, zz] if half is None else self.buf.at[yy, half, zz]
        return self.copies.make(self.first + index, ref, ref, to)

    def ring_id(self, second, block, direction, hop, length):
        base = 0 if not second else (NZ if self.z_first else NY) + block * length
        return base + (0 if direction > 0 else length // 2) + hop - 1

    def along_z(self, second, y_offset, block, direction, hop, sending):
        h = self.here
        distance = hop - 1 if sending else hop
        half = (0 if direction > 0 else 1) if hop == NZ // 2 else None
        return self.copy(
            self.ring_id(second, block, direction, hop, NZ),
            h.y + y_offset,
            h.z - direction * distance,
            half,
            device(h.y, h.x, h.z + direction, h.core),
        )

    def along_y(self, second, z_offset, block, direction, hop, sending):
        h = self.here
        distance = hop - 1 if sending else hop
        half = (0 if direction > 0 else 1) if hop == NY // 2 else None
        return self.copy(
            self.ring_id(second, block, direction, hop, NY),
            h.y - direction * distance,
            h.z + z_offset,
            half,
            device(h.y + direction, h.x, h.z, h.core),
        )

    def first_ring(self, direction, hop, sending):
        along = self.along_z if self.z_first else self.along_y
        return along(False, 0, 0, direction, hop, sending)

    def second_ring(self, block, direction, hop, sending):
        if self.z_first:
            return self.along_y(True, Z_OFFSETS[block], block, direction, hop, sending)
        return self.along_z(True, Y_OFFSETS[block], block, direction, hop, sending)

    def begin(self):
        self.exchanged()
        for direction in (1, -1):
            self.copies.send(self.first_ring(direction, 1, True))
        for direction in (1, -1):
            self.copies.send(self.second_ring(0, direction, 1, True))

    def first_arrival(self, hop):
        half_way = (NZ if self.z_first else NY) // 2
        for turn, direction in enumerate((1, -1)):
            self.first_ring(direction, hop, False).wait_recv()
            if hop < half_way:
                self.copies.send(self.first_ring(direction, hop + 1, True))
                for across in (1, -1):
                    self.copies.send(self.second_ring(2 * hop - 1 + turn, across, 1, True))
        if hop == half_way:
            for across in (1, -1):
                self.copies.send(self.second_ring(2 * hop - 1, across, 1, True))

    def second_arrival(self, block, hop):
        half_way = (NY if self.z_first else NZ) // 2
        for direction in (1, -1):
            self.second_ring(block, direction, hop, False).wait_recv()
            if hop < half_way:
                self.copies.send(self.second_ring(block, direction, hop + 1, True))

    def stages(self):
        blocks, ring, across = (NZ, NZ, NY) if self.z_first else (NY, NY, NZ)
        out = [[self.begin]]
        for hop in range(1, ring // 2 + 1):
            out.append([functools.partial(self.first_arrival, hop)])
        for b in range(blocks):
            for hop in range(1, across // 2):
                at = (b + 1) // 2 + hop
                while len(out) <= at:
                    out.append([])
                out[at].append(functools.partial(self.second_arrival, b, hop))
        return out

    def rest(self):
        blocks, across = (NZ, NY) if self.z_first else (NY, NZ)
        for b in range(blocks):
            self.second_arrival(b, across // 2)


class Columns(Gather):
    def __init__(self, here, copies, buf):
        super().__init__(here, copies, buf, True)

    def across(self, block, direction, hop, sending):
        h = self.here
        return self.copy(
            self.ring_id(True, block, direction, hop, NY),
            h.y - direction * (hop - 1 if sending else hop),
            h.z + Z_OFFSETS[block],
            None,
            device(h.y + direction, h.x, h.z, h.core),
        )

    def ring_begin(self):
        self.exchanged()
        for direction in (1, -1):
            self.copies.send(self.first_ring(direction, 1, True))

    def ring_arrival(self, hop):
        for direction in (1, -1):
            self.first_ring(direction, hop, False).wait_recv()
            if hop < NZ // 2:
                self.copies.send(self.first_ring(direction, hop + 1, True))

    def send_across(self, direction, blocks=range(NZ)):
        for block in blocks:
            self.copies.send(self.across(block, direction, 1, True))

    def pass_across(self, blocks):
        for block in blocks:
            self.across(block, -1, 1, False).wait_recv()
            self.copies.send(self.across(block, -1, 2, True))

    def await_tile(self, tile):
        if tile >= 2:
            for block in range(NZ):
                self.across(block, 1 if tile == 2 else -1, tile - 1 if tile == 2 else 2, False).wait_recv()


class Tokens:
    def __init__(self, here, copies, rows):
        self.here, self.copies, self.rows = here, copies, rows
        self.first = copies.reserve(13)

    def part(self, x, core, half):
        x = lax.rem(x + RING_X, RING_X)
        ref = self.rows.at[lax.rem(x, 2), (x // 2) * 2 + core]
        return ref if half is None else ref.at[pl.ds(half * (BLOCK // 2), BLOCK // 2)]

    def ring(self, direction, hop, half, sending):
        h = self.here
        index = (0 if direction > 0 else 2) + half if hop == 1 else 4 + half
        ref = self.part(h.x - direction * (hop - 1 if sending else hop), h.core, half)
        return self.copies.make(self.first + index, ref, ref, device(h.y, h.x + direction, h.z, h.core))

    def beside(self, distance, half, sending):
        h = self.here
        index = 6 if half is None else {-1: 7, 1: 9, 2: 11}[distance] + half
        ref = self.part(h.x + distance, h.core if sending else 1 - h.core, half)
        return self.copies.make(self.first + index, ref, ref, device(h.y, h.x, h.z, 1 - h.core))

    def begin(self):
        for turn in (0, 1):
            self.copies.send(self.ring(1, 1, turn, True))
            self.copies.send(self.ring(-1, 1, 1 - turn, True))
        self.copies.send(self.beside(0, None, True))

    def first_hop(self, turn):
        for direction in (1, -1):
            half = turn if direction > 0 else 1 - turn
            self.ring(direction, 1, half, False).wait_recv()
            if turn == 0:
                self.copies.send(self.ring(direction, 2, half, True))
            self.copies.send(self.beside(-direction, half, True))

    def second_hop(self):
        for direction, half in ((1, 0), (-1, 1)):
            self.ring(direction, 2, half, False).wait_recv()
            self.copies.send(self.beside(2, half, True))

    def rest(self):
        self.beside(0, None, False).wait_recv()
        for distance in (-1, 1, 2):
            for half in (0, 1):
                self.beside(distance, half, False).wait_recv()


class Relay:
    def __init__(self, here, copies, kv, hops):
        self.here, self.copies, self.kv, self.hops = here, copies, kv, hops
        self.first = copies.reserve(RELAY_COPIES)
        self.count = kv.shape[2] // SPAN

    def rows(self, distance, offset=0):
        skipped = BLOCK if distance == SPAN - 1 else 0
        return pl.ds(offset + skipped, self.count - skipped)

    def slot(self, kind, distance, xl):
        return self.kv.at[kind, xl, self.rows(distance, (SPAN - 1 - distance) * self.count)]

    def hop(self, distance, xl, needed=None):
        rows = self.rows(distance if needed is None else needed)
        return self.hops.at[distance - 1, xl, rows]

    def along(self, distance, xl):
        h = self.here
        if distance > 1:
            src = self.hop(distance - 1, xl, distance)
        else:
            src = self.slot(h.core, 0, xl)
        return self.copies.make(
            self.first + 2 * (distance - 1) + xl, src, self.hop(distance, xl), device(h.y, h.x, h.z + 1, h.core)
        )

    def over(self, distance):
        h = self.here
        return self.copies.make(
            self.first + 5 + distance,
            self.hop(distance, 1),
            self.slot(h.core, distance, 0),
            device(h.y + 1, h.x, h.z, h.core),
        )

    def beside(self, distance, xl, sending):
        h = self.here
        ref = self.slot(h.core if sending else 1 - h.core, distance, xl)
        return self.copies.make(
            self.first + 9 + 2 * distance + xl, ref, ref, device(h.y, h.x, h.z, 1 - h.core)
        )

    def begin(self, xl):
        self.copies.send(self.along(1, xl))
        self.copies.send(self.beside(0, xl, True))

    def place(self, distance, xl, source):
        at = self.rows(distance, (SPAN - 1 - distance) * self.count)
        self.kv[self.here.core, xl, at] = self.hops[distance - 1, source, self.rows(distance)]

    def arrival(self, distance, xl):
        wrapped = self.here.z < distance
        self.along(distance, xl).wait_recv()
        if distance < SPAN - 1:
            self.copies.send(self.along(distance + 1, xl))
        if xl == 1:
            self.copies.send(self.over(distance), wrapped)
            pl.when(jnp.logical_not(wrapped))(lambda: self.place(distance, 1, 1))
        else:
            pl.when(wrapped)(lambda: self.place(distance, 1, 0))
            pl.when(jnp.logical_not(wrapped))(lambda: self.place(distance, 0, 0))
            self.copies.send(self.beside(distance, 1, True))

    def placed(self, distance):
        pl.when(self.here.z < distance)(self.over(distance).wait_recv)
        self.copies.send(self.beside(distance, 0, True))

    def rest(self):
        for distance in range(SPAN):
            for xl in range(NX):
                self.beside(distance, xl, False).wait_recv()


class Products:
    def __init__(self, here, copies, own, other, part_a, part_b, whole_a, whole_b):
        self.here, self.copies, self.own, self.other = here, copies, own, other
        self.half_way = {1: part_a, -1: part_b}
        self.whole = {1: whole_a, -1: whole_b}
        self.first = copies.reserve(PRODUCT_COPIES)
        self.width = own.shape[-1]

    def columns(self, tile, half):
        y = lax.rem(self.here.y + TILE_OFFSETS[tile] + NY, NY)
        return pl.ds(pl.multiple_of((2 * y + half) * self.width, self.width), self.width)

    def beside(self, tile, j, half):
        h = self.here
        return self.copies.make(
            self.first + 14 * tile + 6 + 2 * j + half,
            self.own.at[1 - h.core, j, 2 * tile + half],
            self.other.at[j, 2 * tile + half],
            device(h.y, h.x, h.z, 1 - h.core),
        )

    def far_place(self, tile, direction):
        return self.half_way[direction].at[tile]

    def far(self, tile, direction):
        h = self.here
        half = 0 if direction > 0 else 1
        return self.copies.make(
            self.first + 14 * tile + half,
            self.own.at[h.core, 0, 2 * tile + half],
            self.far_place(tile, direction),
            device(h.y, h.x + direction, h.z, h.core),
        )

    def near(self, tile, direction, half):
        h = self.here
        j = 1 if direction > 0 else 2
        return self.copies.make(
            self.first + 14 * tile + 2 * j + half,
            self.own.at[h.core, j, 2 * tile + half],
            self.whole[direction].at[2 * tile + half],
            device(h.y, h.x + direction, h.z, h.core),
        )

    def add(self, tile, j, half, more=None):
        h = self.here
        at = 2 * tile + half
        total = self.own[h.core, j, at].astype(jnp.float32) + self.other[j, at].astype(jnp.float32)
        if more is not None:
            total = total + more[...].astype(jnp.float32)
        self.own[h.core, j, at] = total.astype(jnp.bfloat16)

    def reduce(self, tile, j):
        order = (1, 0) if j == 1 else (0, 1)
        for turn, half in enumerate(order):
            self.beside(tile, j, half).wait_recv()
            if j == 0:
                self.add(tile, 0, half)
                self.copies.send(self.far(tile, 1 if half == 0 else -1))
            elif j < 3 and turn == 0:
                self.add(tile, j, half)
                self.copies.send(self.near(tile, 1 if j == 1 else -1, half))

    def pass_on(self, tile):
        for direction in (1, -1):
            j, half = (1, 0) if direction > 0 else (2, 1)
            self.far(tile, direction).wait_recv()
            self.add(tile, j, half, self.far_place(tile, direction))
            self.copies.send(self.near(tile, direction, half))

    def last(self, tile, out):
        h = self.here
        for half in (0, 1):
            for direction in (1, -1):
                self.near(tile, direction, half).wait_recv()
        for half in (0, 1):
            at = 2 * tile + half
            total = self.own[h.core, 3, at].astype(jnp.float32) + self.other[3, at].astype(jnp.float32)
            for direction in (1, -1):
                total = total + self.whole[direction][at].astype(jnp.float32)
            out[:, self.columns(tile, half)] = total.astype(out.dtype)


def neighbours(h):
    outer = h.x - 1 + 2 * h.xl
    return [
        device(h.y, h.x, h.z, 1 - h.core),
        device(h.y, h.xh * 2 + 1 - h.xl, h.z, h.core),
        device(h.y, h.xh * 2 + 1 - h.xl, h.z, 1 - h.core),
        device(h.y, outer, h.z, h.core),
        device(h.y + 1, h.x, h.z, h.core),
        device(h.y - 1, h.x, h.z, h.core),
        device(h.y, h.x, h.z + 1, h.core),
        device(h.y, h.x, h.z - 1, h.core),
    ]


def block_kernel(
    docs, tokens, gain, wq, wk, wv, wo, inner_cos, inner_sin, outer_cos, outer_sin, out,
    rows, qa, qb, qb_own, oa, queries, kv, values, hops, attended,
    own, other, part_a, part_b, whole_a, whole_b, cosine, sine, bias, send_sems, recv_sems,
):
    h = Place()
    half_heads = wq.shape[1] // 2
    barrier = pltpu.get_barrier_semaphore()
    greeted = neighbours(h)
    for to in greeted:
        pl.semaphore_signal(barrier, inc=1, device_id=to, device_id_type=MESH)

    for p, kind in ((0, wk), (1, wv)):
        qb_own[p, :, :HD] = wq[:, p * half_heads + Q_A : (p + 1) * half_heads]
        qb_own[p, :, HD:] = kind[...]

    copies = Copies(send_sems, recv_sems)
    gathers = [Gather(h, copies, buf, z_first) for buf, z_first in ((qa, True), (qb, False))]
    columns = Columns(h, copies, oa)
    token_rows = Tokens(h, copies, rows)
    relay = Relay(h, copies, kv, hops)
    products = Products(h, copies, own, other, part_a, part_b, whole_a, whole_b)

    def norm(step, _):
        at = pl.ds(pl.multiple_of(step * 32, 32), 32)
        value = tokens[at, :].astype(jnp.float32)
        scale = lax.rsqrt(jnp.mean(value * value, axis=-1, keepdims=True) + 1e-05)
        rows[h.xl, h.xh * 2 + h.core, at, :] = (value * scale * gain[...]).astype(jnp.bfloat16)
        return 0

    lax.fori_loop(0, BLOCK // 32, norm, 0)
    pl.semaphore_wait(barrier, len(greeted))
    gathers[0].exchange([wq.at[:, pl.ds(p * half_heads, Q_A)] for p in (0, 1)])
    gathers[1].exchange([qb_own.at[p] for p in (0, 1)])
    columns.exchange([wo.at[:, pl.ds(p * half_heads, half_heads)] for p in (0, 1)])

    token_rows.begin()

    plans = [part.stages() for part in gathers]

    def run(stage):
        for plan in plans:
            if stage < len(plan):
                for step in plan[stage]:
                    step()

    def fill_tables():
        for xl in range(NX):
            context = (h.y * NX + xl) * NZ + h.z
            oc, os_ = outer_cos[context], outer_sin[context]
            cosine[xl] = inner_cos[...] * oc - inner_sin[...] * os_
            turned = inner_sin[...] * oc + inner_cos[...] * os_
            lane = lax.broadcasted_iota(jnp.int32, turned.shape, 1)
            sine[xl] = jnp.where(lane < HD // 2, -turned, turned)

        def mask(index, _):
            block = ((h.y * NX + index // NTP) * NZ + h.z) * NTP + lax.rem(index, NTP)
            for w in range(WINDOW):
                key = block - (WINDOW - 1) + w
                same = docs[lax.rem(key + docs.shape[0], docs.shape[0])] == docs[block]
                visible = jnp.logical_and(same, key >= 0)
                bias[index, :, w * BLOCK : (w + 1) * BLOCK] = jnp.full(
                    (1, BLOCK), jnp.where(visible, 0.0, neg_large), jnp.float32
                )
            return 0

        lax.fori_loop(0, NX * NTP, mask, 0)
        values[:, :, HD:] = jnp.ones_like(values[:, :, HD:])

    for stage in range(max(len(plan) for plan in plans)):
        run(stage)
        if stage == 0:
            fill_tables()
        if stage == 1:
            columns.ring_begin()
        if stage == 2:
            token_rows.first_hop(0)
        if stage >= 3:
            columns.ring_arrival(stage - 2)
        if stage == 5:
            token_rows.first_hop(1)
    gathers[0].rest()
    gathers[1].rest()
    columns.send_across(-1, range(7))
    token_rows.second_hop()
    token_rows.rest()

    def project(weights, chip):
        at = pl.ds((chip // 2) * 2, 2)
        total = None
        depth = NX * NZ * weights.shape[3]
        for y in range(NY):
            left = rows[lax.rem(chip, 2), at, :, y * depth : (y + 1) * depth].reshape(2 * BLOCK, depth)
            term = jnp.dot(left, weights[y].reshape(depth, weights.shape[4]), preferred_element_type=jnp.float32)
            total = term if total is None else total + term
        return total

    def rotated(value, chip):
        at = pl.ds(pl.multiple_of((chip // 2) * (2 * BLOCK), 2 * BLOCK), 2 * BLOCK)
        swapped = pltpu.roll(value, HD // 2, 1)
        return value * cosine[lax.rem(chip, 2), at, :] + swapped * sine[lax.rem(chip, 2), at, :]

    def keep_query(value, chip, head):
        query = (rotated(value, chip) * HD ** (-0.5)).astype(jnp.bfloat16)
        for core in (0, 1):
            queries[lax.rem(chip, 2), (chip // 2) * 2 + core, head * BLOCK : (head + 1) * BLOCK, :] = query[
                core * BLOCK : (core + 1) * BLOCK
            ]

    def project_b(chip, _):
        total = project(qb, chip)
        keep_query(total[:, :HD], chip, 3)
        value = total[:, HD:]
        value = jnp.where(h.core == 0, rotated(value, chip), value).astype(jnp.bfloat16)
        start = (SPAN - 1) * NTP * BLOCK + (chip // 2) * (2 * BLOCK)
        kv[h.core, lax.rem(chip, 2), pl.ds(pl.multiple_of(start, 2 * BLOCK), 2 * BLOCK), :] = value
        return 0

    def project_a(chip, _):
        total = project(qa, chip)
        for head in range(3):
            keep_query(total[:, head * HD : (head + 1) * HD], chip, head)
        return 0

    for xl in (1, 0):
        lax.fori_loop(0, RING_X // NX, lambda xh, _: project_b(xh * 2 + xl, 0), 0)
        relay.begin(xl)
    lax.fori_loop(0, RING_X, project_a, 0)
    columns.ring_arrival(4)
    columns.send_across(-1, range(7, NZ))
    for distance in range(1, SPAN):
        for xl in (1, 0):
            relay.arrival(distance, xl)
        if distance > 1:
            relay.placed(distance - 1)
        columns.pass_across(range(2 * distance - 2, 2 * distance))
    relay.placed(SPAN - 1)
    columns.send_across(1)
    relay.rest()

    for xl in range(NX):
        values[xl, :, :HD] = kv[1, xl]

    heads = half_heads // HD
    query_at = lax.broadcasted_iota(jnp.int32, (2 * BLOCK, BLOCK), 0)
    query_at = lax.rem(query_at, BLOCK)
    causal = jnp.where(query_at >= lax.broadcasted_iota(jnp.int32, (2 * BLOCK, BLOCK), 1), 0.0, neg_large)

    def attend(chip):
        xl, first_block = lax.rem(chip, 2), (chip // 2) * 2

        def body(step, _):
            block = first_block + step
            window = pl.ds(pl.multiple_of((block + SPAN * NTP - WINDOW - (NTP - 1)) * BLOCK, BLOCK), WINDOW * BLOCK)
            for pair in range(heads // 2):
                query = queries[xl, block, pair * 2 * BLOCK : (pair + 1) * 2 * BLOCK, :]
                scores = lax.dot_general(query, kv[0, xl, window, :], NT, preferred_element_type=jnp.float32)
                scores = scores + bias[xl * NTP + block]
                near = (WINDOW - 1) * BLOCK
                scores = jnp.concatenate([scores[:, :near], scores[:, near:] + causal], axis=1)
                top = jnp.max(scores, axis=-1, keepdims=True)
                weights = jnp.exp(scores - top).astype(jnp.bfloat16)
                total = jnp.dot(weights, values[xl, window, :], preferred_element_type=jnp.float32)
                result = (total[:, :HD] / total[:, HD:]).astype(jnp.bfloat16)
                for k in range(2):
                    head = pair * 2 + k
                    attended[xl, block, :, head * HD : (head + 1) * HD] = result[k * BLOCK : (k + 1) * BLOCK]
            return 0

        lax.fori_loop(0, 2, body, 0)

    order = (2, 1, 3, 0)

    def multiply(tile, j):
        chip = lax.rem(h.x + order[j], RING_X)
        left = attended[lax.rem(chip, 2), pl.ds((chip // 2) * 2, 2)].reshape(2 * BLOCK, half_heads)
        y = lax.rem(h.y + TILE_OFFSETS[tile] + NY, NY)
        depth = NZ * wo.shape[0]

        for half in (0, 1):
            right = oa[y, half].reshape(depth, half_heads)
            total = lax.dot_general(left, right, NT, preferred_element_type=jnp.float32).astype(jnp.bfloat16)
            for core in (0, 1):
                own[core, j, 2 * tile + half] = total[core * BLOCK : (core + 1) * BLOCK]
            copies.send(products.beside(tile, j, half))

    columns.pass_across(range(6, NZ))
    early = (0, 1)
    for j in range(RING_X):
        attend(lax.rem(h.x + order[j], RING_X))
        for tile in early:
            if j > 1:
                products.reduce(tile, j - 1)
        for tile in early:
            multiply(tile, j)
        if j == 0:
            for tile in early:
                products.reduce(tile, 0)
    for tile in early:
        products.pass_on(tile)
    for tile in early:
        products.reduce(tile, 3)
    for tile in (2, 3):
        columns.await_tile(tile)
        for j in range(RING_X):
            multiply(tile, j)
        products.reduce(tile, 0)
        if tile > 2:
            products.pass_on(tile - 1)
        products.reduce(tile, 1)
        products.reduce(tile, 2)
        products.reduce(tile, 3)
    products.pass_on(NY - 1)
    for tile in range(NY):
        products.last(tile, out)
    copies.finish()


COPIES = 2 * COPIES_A + COPIES_B + 6 + 13 + RELAY_COPIES + PRODUCT_COPIES


def rotation_tables(count):
    half_width = HD // 2
    frequency = np.float32(rope_base) ** (-np.arange(half_width, dtype=np.float32) / np.float32(half_width))
    frequency = np.concatenate([frequency, frequency]).astype(np.float64)
    inner = np.arange(count)[:, None] * frequency
    outer = (np.arange(NY * NX * NZ) * count)[:, None, None] * frequency
    return [f(angle).astype(np.float32) for angle in (inner, outer) for f in (np.cos, np.sin)]


def whole_block(doc_blocks, tokens, gain, w_query, w_key, w_value, w_out_t):
    count, width = tokens.shape
    rows = w_query.shape[0]
    half = w_query.shape[1] // 2
    near = NTP * count
    bf16 = jnp.bfloat16
    vmem = pl.BlockSpec(memory_space=pltpu.VMEM)
    turns = rotation_tables(near)
    return pl.pallas_call(
        block_kernel,
        out_shape=pltpu.VMEM((count, width), bf16),
        in_specs=[pl.BlockSpec(memory_space=pltpu.SMEM)] + [vmem] * 10,
        out_specs=vmem,
        scratch_shapes=[
            pltpu.VMEM((NX, NTP, count, width), bf16),
            pltpu.VMEM((NY, NX, NZ, rows, Q_A), bf16),
            pltpu.VMEM((NY, NX, NZ, rows, half - Q_A + HD), bf16),
            pltpu.VMEM((2, rows, half - Q_A + HD), bf16),
            pltpu.VMEM((NY, NX, NZ, rows, half), bf16),
            pltpu.VMEM((NX, NTP, half // HD * BLOCK, HD), bf16),
            pltpu.VMEM((2, NX, SPAN * near, HD), bf16),
            pltpu.VMEM((NX, SPAN * near, 2 * HD), bf16),
            pltpu.VMEM((SPAN - 1, NX, near, HD), bf16),
            pltpu.VMEM((NX, NTP, count, half), bf16),
            pltpu.VMEM((2, RING_X, 2 * NY, count, width // (2 * NY)), bf16),
            pltpu.VMEM((RING_X, 2 * NY, count, width // (2 * NY)), bf16),
            pltpu.VMEM((NY, count, width // (2 * NY)), bf16),
            pltpu.VMEM((NY, count, width // (2 * NY)), bf16),
            pltpu.VMEM((2 * NY, count, width // (2 * NY)), bf16),
            pltpu.VMEM((2 * NY, count, width // (2 * NY)), bf16),
            pltpu.VMEM((NX, near, HD), jnp.float32),
            pltpu.VMEM((NX, near, HD), jnp.float32),
            pltpu.VMEM((NX * NTP, 1, WINDOW * BLOCK), jnp.float32),
            pltpu.SemaphoreType.DMA((COPIES,)),
            pltpu.SemaphoreType.DMA((COPIES,)),
        ],
        compiler_params=pltpu.CompilerParams(
            collective_id=0, has_side_effects=True, vmem_limit_bytes=54 * 1024 * 1024
        ),
    )(doc_blocks, tokens, gain, w_query, w_key, w_value, w_out_t, *turns)


def local(tokens, norm_gain, w_query, w_key, w_value, w_out, doc_blocks):
    return whole_block(doc_blocks, tokens, norm_gain[None, :], w_query, w_key, w_value, w_out.T)


def solution(mesh):
    return jax.shard_map(
        local,
        mesh=mesh,
        in_specs=(
            P(("ctx", "tp"), None),
            P(),
            P("ctx", "tp"),
            P("ctx", "tp"),
            P("ctx", "tp"),
            P("tp", "ctx"),
            P(),
        ),
        out_specs=P(("ctx", "tp"), None),
        check_vma=False,
    )
```

```python
import functools

import jax
import jax.numpy as jnp
import numpy as np
from jax import lax
from jax.experimental import pallas as pl
from jax.experimental.pallas import tpu as pltpu
from jax.sharding import PartitionSpec as P

HD = 128
BLOCK = 128
WINDOW = 12
SPAN = 4
NY, NX, NZ, NTP = 4, 2, 8, 4
RING_X = 4
MESH = pl.DeviceIdType.MESH

rope_base = 500000.0
neg_large = -1e30

Z_OFFSETS = [0, -1, 1, -2, 2, -3, 3, 4]
Y_OFFSETS = [0, -1, 1, 2]
TILE_OFFSETS = [0, 1, -1, 2]
COPIES_A = 8 + 32
COPIES_B = 4 + 32
RELAY_COPIES = 17
PRODUCT_COPIES = 14 * NY
Q_A = 384
NT = (((1,), (1,)), ((), ()))


class Place:
    def __init__(self):
        c, t = lax.axis_index("ctx"), lax.axis_index("tp")
        self.y, self.xl, self.z = c // (NX * NZ), lax.rem(c // NZ, NX), lax.rem(c, NZ)
        self.xh, self.core = t // 2, lax.rem(t, 2)
        self.x = self.xh * 2 + self.xl


def device(y, x, z, core):
    x = lax.rem(x + RING_X, RING_X)
    ctx = (lax.rem(y + NY, NY) * NX + lax.rem(x, 2)) * NZ + lax.rem(z + NZ, NZ)
    return (ctx, (x // 2) * 2 + core)


class Copies:
    def __init__(self, send_sems, recv_sems):
        self.send_sems, self.recv_sems = send_sems, recv_sems
        self.used = 0
        self.sent = []

    def reserve(self, count):
        first = self.used
        self.used += count
        return first

    def make(self, index, src, dst, to, recv_index=None):
        return pltpu.make_async_remote_copy(
            src_ref=src,
            dst_ref=dst,
            send_sem=self.send_sems.at[index],
            recv_sem=self.recv_sems.at[index if recv_index is None else recv_index],
            device_id=to,
            device_id_type=MESH,
        )

    def send(self, copy, when=None):
        if when is None:
            copy.start()
        else:
            pl.when(when)(copy.start)
        self.sent.append((copy, when))

    def finish(self):
        for copy, when in self.sent:
            if when is None:
                copy.wait_send()
            else:
                pl.when(when)(copy.wait_send)


class Gather:
    def __init__(self, here, copies, buf, z_first):
        self.here, self.copies, self.buf, self.z_first = here, copies, buf, z_first
        self.first = copies.reserve(COPIES_A if z_first else COPIES_B)
        self.arrive = copies.reserve(2)

    def exchange(self, parts):
        h = self.here
        for p in (0, 1):
            local = jnp.logical_and(h.core == h.xl, h.core == p)

            @pl.when(local)
            def _():
                self.buf[h.y, h.xl, h.z] = parts[p][...]

            copy = self.copies.make(
                self.arrive + p,
                parts[p],
                self.buf.at[h.y, h.xl, h.z],
                device(h.y, h.xh * 2 + h.core, h.z, p),
                self.arrive + h.xl,
            )
            self.copies.send(copy, jnp.logical_not(local))

    def exchanged(self):
        h = self.here
        for slot in (0, 1):
            local = jnp.logical_and(h.core == h.xl, h.xl == slot)
            ref = self.buf.at[h.y, slot, h.z]
            copy = self.copies.make(self.arrive + slot, ref, ref, device(h.y, h.x + 1, h.z, h.core))
            pl.when(jnp.logical_not(local))(copy.wait_recv)

    def copy(self, index, yy, zz, half, to):
        yy, zz = lax.rem(yy + 2 * NY, NY), lax.rem(zz + 2 * NZ, NZ)
        ref = self.buf.at[yy, :, zz] if half is None else self.buf.at[yy, half, zz]
        return self.copies.make(self.first + index, ref, ref, to)

    def ring_id(self, second, block, direction, hop, length):
        base = 0 if not second else (NZ if self.z_first else NY) + block * length
        return base + (0 if direction > 0 else length // 2) + hop - 1

    def along_z(self, second, y_offset, block, direction, hop, sending):
        h = self.here
        distance = hop - 1 if sending else hop
        half = (0 if direction > 0 else 1) if hop == NZ // 2 else None
        return self.copy(
            self.ring_id(second, block, direction, hop, NZ),
            h.y + y_offset,
            h.z - direction * distance,
            half,
            device(h.y, h.x, h.z + direction, h.core),
        )

    def along_y(self, second, z_offset, block, direction, hop, sending):
        h = self.here
        distance = hop - 1 if sending else hop
        half = (0 if direction > 0 else 1) if hop == NY // 2 else None
        return self.copy(
            self.ring_id(second, block, direction, hop, NY),
            h.y - direction * distance,
            h.z + z_offset,
            half,
            device(h.y + direction, h.x, h.z, h.core),
        )

    def first_ring(self, direction, hop, sending):
        along = self.along_z if self.z_first else self.along_y
        return along(False, 0, 0, direction, hop, sending)

    def second_ring(self, block, direction, hop, sending):
        if self.z_first:
            return self.along_y(True, Z_OFFSETS[block], block, direction, hop, sending)
        return self.along_z(True, Y_OFFSETS[block], block, direction, hop, sending)

    def begin(self):
        self.exchanged()
        for direction in (1, -1):
            self.copies.send(self.first_ring(direction, 1, True))
        for direction in (1, -1):
            self.copies.send(self.second_ring(0, direction, 1, True))

    def first_arrival(self, hop):
        half_way = (NZ if self.z_first else NY) // 2
        for turn, direction in enumerate((1, -1)):
            self.first_ring(direction, hop, False).wait_recv()
            if hop < half_way:
                self.copies.send(self.first_ring(direction, hop + 1, True))
                for across in (1, -1):
                    self.copies.send(self.second_ring(2 * hop - 1 + turn, across, 1, True))
        if hop == half_way:
            for across in (1, -1):
                self.copies.send(self.second_ring(2 * hop - 1, across, 1, True))

    def second_arrival(self, block, hop):
        half_way = (NY if self.z_first else NZ) // 2
        for direction in (1, -1):
            self.second_ring(block, direction, hop, False).wait_recv()
            if hop < half_way:
                self.copies.send(self.second_ring(block, direction, hop + 1, True))

    def stages(self):
        blocks, ring, across = (NZ, NZ, NY) if self.z_first else (NY, NY, NZ)
        out = [[self.begin]]
        for hop in range(1, ring // 2 + 1):
            out.append([functools.partial(self.first_arrival, hop)])
        for b in range(blocks):
            for hop in range(1, across // 2):
                at = (b + 1) // 2 + hop
                while len(out) <= at:
                    out.append([])
                out[at].append(functools.partial(self.second_arrival, b, hop))
        return out

    def rest(self):
        blocks, across = (NZ, NY) if self.z_first else (NY, NZ)
        for b in range(blocks):
            self.second_arrival(b, across // 2)


class Columns(Gather):
    def __init__(self, here, copies, buf):
        super().__init__(here, copies, buf, True)

    def across(self, block, direction, hop, sending):
        h = self.here
        return self.copy(
            self.ring_id(True, block, direction, hop, NY),
            h.y - direction * (hop - 1 if sending else hop),
            h.z + Z_OFFSETS[block],
            None,
            device(h.y + direction, h.x, h.z, h.core),
        )

    def ring_begin(self):
        self.exchanged()
        for direction in (1, -1):
            self.copies.send(self.first_ring(direction, 1, True))

    def ring_arrival(self, hop):
        for direction in (1, -1):
            self.first_ring(direction, hop, False).wait_recv()
            if hop < NZ // 2:
                self.copies.send(self.first_ring(direction, hop + 1, True))

    def send_across(self, direction, blocks=range(NZ)):
        for block in blocks:
            self.copies.send(self.across(block, direction, 1, True))

    def pass_across(self, blocks):
        for block in blocks:
            self.across(block, -1, 1, False).wait_recv()
            self.copies.send(self.across(block, -1, 2, True))

    def await_tile(self, tile):
        if tile >= 2:
            for block in range(NZ):
                self.across(block, 1 if tile == 2 else -1, tile - 1 if tile == 2 else 2, False).wait_recv()


class Tokens:
    def __init__(self, here, copies, rows):
        self.here, self.copies, self.rows = here, copies, rows
        self.first = copies.reserve(13)

    def part(self, x, core, half):
        x = lax.rem(x + RING_X, RING_X)
        ref = self.rows.at[lax.rem(x, 2), (x // 2) * 2 + core]
        return ref if half is None else ref.at[pl.ds(half * (BLOCK // 2), BLOCK // 2)]

    def ring(self, direction, hop, half, sending):
        h = self.here
        index = (0 if direction > 0 else 2) + half if hop == 1 else 4 + half
        ref = self.part(h.x - direction * (hop - 1 if sending else hop), h.core, half)
        return self.copies.make(self.first + index, ref, ref, device(h.y, h.x + direction, h.z, h.core))

    def beside(self, distance, half, sending):
        h = self.here
        index = 6 if half is None else {-1: 7, 1: 9, 2: 11}[distance] + half
        ref = self.part(h.x + distance, h.core if sending else 1 - h.core, half)
        return self.copies.make(self.first + index, ref, ref, device(h.y, h.x, h.z, 1 - h.core))

    def begin(self):
        for turn in (0, 1):
            self.copies.send(self.ring(1, 1, turn, True))
            self.copies.send(self.ring(-1, 1, 1 - turn, True))
        self.copies.send(self.beside(0, None, True))

    def first_hop(self, turn):
        for direction in (1, -1):
            half = turn if direction > 0 else 1 - turn
            self.ring(direction, 1, half, False).wait_recv()
            if turn == 0:
                self.copies.send(self.ring(direction, 2, half, True))
            self.copies.send(self.beside(-direction, half, True))

    def second_hop(self):
        for direction, half in ((1, 0), (-1, 1)):
            self.ring(direction, 2, half, False).wait_recv()
            self.copies.send(self.beside(2, half, True))

    def rest(self):
        self.beside(0, None, False).wait_recv()
        for distance in (-1, 1, 2):
            for half in (0, 1):
                self.beside(distance, half, False).wait_recv()


class Relay:
    def __init__(self, here, copies, kv, hops):
        self.here, self.copies, self.kv, self.hops = here, copies, kv, hops
        self.first = copies.reserve(RELAY_COPIES)
        self.count = kv.shape[2] // SPAN

    def rows(self, distance, offset=0):
        skipped = BLOCK if distance == SPAN - 1 else 0
        return pl.ds(offset + skipped, self.count - skipped)

    def slot(self, kind, distance, xl):
        return self.kv.at[kind, xl, self.rows(distance, (SPAN - 1 - distance) * self.count)]

    def hop(self, distance, xl, needed=None):
        rows = self.rows(distance if needed is None else needed)
        return self.hops.at[distance - 1, xl, rows]

    def along(self, distance, xl):
        h = self.here
        if distance > 1:
            src = self.hop(distance - 1, xl, distance)
        else:
            src = self.slot(h.core, 0, xl)
        return self.copies.make(
            self.first + 2 * (distance - 1) + xl, src, self.hop(distance, xl), device(h.y, h.x, h.z + 1, h.core)
        )

    def over(self, distance):
        h = self.here
        return self.copies.make(
            self.first + 5 + distance,
            self.hop(distance, 1),
            self.slot(h.core, distance, 0),
            device(h.y + 1, h.x, h.z, h.core),
        )

    def beside(self, distance, xl, sending):
        h = self.here
        ref = self.slot(h.core if sending else 1 - h.core, distance, xl)
        return self.copies.make(
            self.first + 9 + 2 * distance + xl, ref, ref, device(h.y, h.x, h.z, 1 - h.core)
        )

    def begin(self, xl):
        self.copies.send(self.along(1, xl))
        self.copies.send(self.beside(0, xl, True))

    def place(self, distance, xl, source):
        at = self.rows(distance, (SPAN - 1 - distance) * self.count)
        self.kv[self.here.core, xl, at] = self.hops[distance - 1, source, self.rows(distance)]

    def arrival(self, distance, xl):
        wrapped = self.here.z < distance
        self.along(distance, xl).wait_recv()
        if distance < SPAN - 1:
            self.copies.send(self.along(distance + 1, xl))
        if xl == 1:
            self.copies.send(self.over(distance), wrapped)
            pl.when(jnp.logical_not(wrapped))(lambda: self.place(distance, 1, 1))
        else:
            pl.when(wrapped)(lambda: self.place(distance, 1, 0))
            pl.when(jnp.logical_not(wrapped))(lambda: self.place(distance, 0, 0))
            self.copies.send(self.beside(distance, 1, True))

    def placed(self, distance):
        pl.when(self.here.z < distance)(self.over(distance).wait_recv)
        self.copies.send(self.beside(distance, 0, True))

    def rest(self):
        for distance in range(SPAN):
            for xl in range(NX):
                self.beside(distance, xl, False).wait_recv()


class Products:
    def __init__(self, here, copies, own, other, part_a, part_b, whole_a, whole_b):
        self.here, self.copies, self.own, self.other = here, copies, own, other
        self.half_way = {1: part_a, -1: part_b}
        self.whole = {1: whole_a, -1: whole_b}
        self.first = copies.reserve(PRODUCT_COPIES)
        self.width = own.shape[-1]

    def columns(self, tile, half):
        y = lax.rem(self.here.y + TILE_OFFSETS[tile] + NY, NY)
        return pl.ds(pl.multiple_of((2 * y + half) * self.width, self.width), self.width)

    def beside(self, tile, j, half):
        h = self.here
        return self.copies.make(
            self.first + 14 * tile + 6 + 2 * j + half,
            self.own.at[1 - h.core, j, 2 * tile + half],
            self.other.at[j, 2 * tile + half],
            device(h.y, h.x, h.z, 1 - h.core),
        )

    def far_place(self, tile, direction):
        return self.half_way[direction].at[tile]

    def far(self, tile, direction):
        h = self.here
        half = 0 if direction > 0 else 1
        return self.copies.make(
            self.first + 14 * tile + half,
            self.own.at[h.core, 0, 2 * tile + half],
            self.far_place(tile, direction),
            device(h.y, h.x + direction, h.z, h.core),
        )

    def near(self, tile, direction, half):
        h = self.here
        j = 1 if direction > 0 else 2
        return self.copies.make(
            self.first + 14 * tile + 2 * j + half,
            self.own.at[h.core, j, 2 * tile + half],
            self.whole[direction].at[2 * tile + half],
            device(h.y, h.x + direction, h.z, h.core),
        )

    def add(self, tile, j, half, more=None):
        h = self.here
        at = 2 * tile + half
        total = self.own[h.core, j, at].astype(jnp.float32) + self.other[j, at].astype(jnp.float32)
        if more is not None:
            total = total + more[...].astype(jnp.float32)
        self.own[h.core, j, at] = total.astype(jnp.bfloat16)

    def reduce(self, tile, j):
        order = (1, 0) if j == 1 else (0, 1)
        for turn, half in enumerate(order):
            self.beside(tile, j, half).wait_recv()
            if j == 0:
                self.add(tile, 0, half)
                self.copies.send(self.far(tile, 1 if half == 0 else -1))
            elif j < 3 and turn == 0:
                self.add(tile, j, half)
                self.copies.send(self.near(tile, 1 if j == 1 else -1, half))

    def pass_on(self, tile):
        for direction in (1, -1):
            j, half = (1, 0) if direction > 0 else (2, 1)
            self.far(tile, direction).wait_recv()
            self.add(tile, j, half, self.far_place(tile, direction))
            self.copies.send(self.near(tile, direction, half))

    def last(self, tile, out):
        h = self.here
        for half in (0, 1):
            for direction in (1, -1):
                self.near(tile, direction, half).wait_recv()
        for half in (0, 1):
            at = 2 * tile + half
            total = self.own[h.core, 3, at].astype(jnp.float32) + self.other[3, at].astype(jnp.float32)
            for direction in (1, -1):
                total = total + self.whole[direction][at].astype(jnp.float32)
            out[:, self.columns(tile, half)] = total.astype(out.dtype)


def neighbours(h):
    outer = h.x - 1 + 2 * h.xl
    return [
        device(h.y, h.x, h.z, 1 - h.core),
        device(h.y, h.xh * 2 + 1 - h.xl, h.z, h.core),
        device(h.y, h.xh * 2 + 1 - h.xl, h.z, 1 - h.core),
        device(h.y, outer, h.z, h.core),
        device(h.y + 1, h.x, h.z, h.core),
        device(h.y - 1, h.x, h.z, h.core),
        device(h.y, h.x, h.z + 1, h.core),
        device(h.y, h.x, h.z - 1, h.core),
    ]


def block_kernel(
    docs, tokens, gain, wq, wk, wv, wo, inner_cos, inner_sin, outer_cos, outer_sin, out,
    rows, qa, qb, qb_own, oa, queries, kv, values, hops, attended,
    own, other, part_a, part_b, whole_a, whole_b, cosine, sine, bias, send_sems, recv_sems,
):
    h = Place()
    half_heads = wq.shape[1] // 2
    barrier = pltpu.get_barrier_semaphore()
    greeted = neighbours(h)
    for to in greeted:
        pl.semaphore_signal(barrier, inc=1, device_id=to, device_id_type=MESH)

    for p, kind in ((0, wk), (1, wv)):
        qb_own[p, :, :HD] = wq[:, p * half_heads + Q_A : (p + 1) * half_heads]
        qb_own[p, :, HD:] = kind[...]

    copies = Copies(send_sems, recv_sems)
    gathers = [Gather(h, copies, buf, z_first) for buf, z_first in ((qa, True), (qb, False))]
    columns = Columns(h, copies, oa)
    token_rows = Tokens(h, copies, rows)
    relay = Relay(h, copies, kv, hops)
    products = Products(h, copies, own, other, part_a, part_b, whole_a, whole_b)

    def norm(step, _):
        at = pl.ds(pl.multiple_of(step * 32, 32), 32)
        value = tokens[at, :].astype(jnp.float32)
        scale = lax.rsqrt(jnp.mean(value * value, axis=-1, keepdims=True) + 1e-05)
        rows[h.xl, h.xh * 2 + h.core, at, :] = (value * scale * gain[...]).astype(jnp.bfloat16)
        return 0

    lax.fori_loop(0, BLOCK // 32, norm, 0)
    pl.semaphore_wait(barrier, len(greeted))
    gathers[0].exchange([wq.at[:, pl.ds(p * half_heads, Q_A)] for p in (0, 1)])
    gathers[1].exchange([qb_own.at[p] for p in (0, 1)])
    columns.exchange([wo.at[:, pl.ds(p * half_heads, half_heads)] for p in (0, 1)])

    token_rows.begin()

    plans = [part.stages() for part in gathers]

    def run(stage):
        for plan in plans:
            if stage < len(plan):
                for step in plan[stage]:
                    step()

    def fill_tables():
        for xl in range(NX):
            context = (h.y * NX + xl) * NZ + h.z
            oc, os_ = outer_cos[context], outer_sin[context]
            cosine[xl] = inner_cos[...] * oc - inner_sin[...] * os_
            turned = inner_sin[...] * oc + inner_cos[...] * os_
            lane = lax.broadcasted_iota(jnp.int32, turned.shape, 1)
            sine[xl] = jnp.where(lane < HD // 2, -turned, turned)

        def mask(index, _):
            block = ((h.y * NX + index // NTP) * NZ + h.z) * NTP + lax.rem(index, NTP)
            for w in range(WINDOW):
                key = block - (WINDOW - 1) + w
                same = docs[lax.rem(key + docs.shape[0], docs.shape[0])] == docs[block]
                visible = jnp.logical_and(same, key >= 0)
                bias[index, :, w * BLOCK : (w + 1) * BLOCK] = jnp.full(
                    (1, BLOCK), jnp.where(visible, 0.0, neg_large), jnp.float32
                )
            return 0

        lax.fori_loop(0, NX * NTP, mask, 0)
        values[:, :, HD:] = jnp.ones_like(values[:, :, HD:])

    for stage in range(max(len(plan) for plan in plans)):
        run(stage)
        if stage == 1:
            columns.ring_begin()
        if stage == 2:
            token_rows.first_hop(0)
        if stage >= 3:
            columns.ring_arrival(stage - 2)
        if stage == 5:
            token_rows.first_hop(1)
    gathers[0].rest()
    gathers[1].rest()
    columns.send_across(-1, range(7))
    fill_tables()
    token_rows.second_hop()
    token_rows.rest()

    def project(weights, chip):
        at = pl.ds((chip // 2) * 2, 2)
        total = None
        depth = NX * NZ * weights.shape[3]
        for y in range(NY):
            left = rows[lax.rem(chip, 2), at, :, y * depth : (y + 1) * depth].reshape(2 * BLOCK, depth)
            term = jnp.dot(left, weights[y].reshape(depth, weights.shape[4]), preferred_element_type=jnp.float32)
            total = term if total is None else total + term
        return total

    def rotated(value, chip):
        at = pl.ds(pl.multiple_of((chip // 2) * (2 * BLOCK), 2 * BLOCK), 2 * BLOCK)
        swapped = pltpu.roll(value, HD // 2, 1)
        return value * cosine[lax.rem(chip, 2), at, :] + swapped * sine[lax.rem(chip, 2), at, :]

    def keep_query(value, chip, head):
        query = (rotated(value, chip) * HD ** (-0.5)).astype(jnp.bfloat16)
        for core in (0, 1):
            queries[lax.rem(chip, 2), (chip // 2) * 2 + core, head * BLOCK : (head + 1) * BLOCK, :] = query[
                core * BLOCK : (core + 1) * BLOCK
            ]

    def project_b(chip, _):
        total = project(qb, chip)
        keep_query(total[:, :HD], chip, 3)
        value = total[:, HD:]
        value = jnp.where(h.core == 0, rotated(value, chip), value).astype(jnp.bfloat16)
        start = (SPAN - 1) * NTP * BLOCK + (chip // 2) * (2 * BLOCK)
        kv[h.core, lax.rem(chip, 2), pl.ds(pl.multiple_of(start, 2 * BLOCK), 2 * BLOCK), :] = value
        return 0

    def project_a(chip, _):
        total = project(qa, chip)
        for head in range(3):
            keep_query(total[:, head * HD : (head + 1) * HD], chip, head)
        return 0

    for xl in (1, 0):
        lax.fori_loop(0, RING_X // NX, lambda xh, _: project_b(xh * 2 + xl, 0), 0)
        relay.begin(xl)
    lax.fori_loop(0, RING_X, project_a, 0)
    columns.ring_arrival(4)
    columns.send_across(-1, range(7, NZ))
    for distance in range(1, SPAN):
        for xl in (1, 0):
            relay.arrival(distance, xl)
        if distance > 1:
            relay.placed(distance - 1)
        columns.pass_across(range(2 * distance - 2, 2 * distance))
    relay.placed(SPAN - 1)
    columns.send_across(1)
    relay.rest()

    for xl in range(NX):
        values[xl, :, :HD] = kv[1, xl]

    heads = half_heads // HD
    query_at = lax.broadcasted_iota(jnp.int32, (2 * BLOCK, BLOCK), 0)
    query_at = lax.rem(query_at, BLOCK)
    causal = jnp.where(query_at >= lax.broadcasted_iota(jnp.int32, (2 * BLOCK, BLOCK), 1), 0.0, neg_large)

    def attend(chip):
        xl, first_block = lax.rem(chip, 2), (chip // 2) * 2

        def body(step, _):
            block = first_block + step
            window = pl.ds(pl.multiple_of((block + SPAN * NTP - WINDOW - (NTP - 1)) * BLOCK, BLOCK), WINDOW * BLOCK)
            for pair in range(heads // 2):
                query = queries[xl, block, pair * 2 * BLOCK : (pair + 1) * 2 * BLOCK, :]
                scores = lax.dot_general(query, kv[0, xl, window, :], NT, preferred_element_type=jnp.float32)
                scores = scores + bias[xl * NTP + block]
                near = (WINDOW - 1) * BLOCK
                scores = jnp.concatenate([scores[:, :near], scores[:, near:] + causal], axis=1)
                top = jnp.max(scores, axis=-1, keepdims=True)
                weights = jnp.exp(scores - top).astype(jnp.bfloat16)
                total = jnp.dot(weights, values[xl, window, :], preferred_element_type=jnp.float32)
                result = (total[:, :HD] / total[:, HD:]).astype(jnp.bfloat16)
                for k in range(2):
                    head = pair * 2 + k
                    attended[xl, block, :, head * HD : (head + 1) * HD] = result[k * BLOCK : (k + 1) * BLOCK]
            return 0

        lax.fori_loop(0, 2, body, 0)

    order = (2, 1, 3, 0)

    def multiply(tile, j):
        chip = lax.rem(h.x + order[j], RING_X)
        left = attended[lax.rem(chip, 2), pl.ds((chip // 2) * 2, 2)].reshape(2 * BLOCK, half_heads)
        y = lax.rem(h.y + TILE_OFFSETS[tile] + NY, NY)
        depth = NZ * wo.shape[0]

        for half in (0, 1):
            right = oa[y, half].reshape(depth, half_heads)
            total = lax.dot_general(left, right, NT, preferred_element_type=jnp.float32).astype(jnp.bfloat16)
            for core in (0, 1):
                own[core, j, 2 * tile + half] = total[core * BLOCK : (core + 1) * BLOCK]
            copies.send(products.beside(tile, j, half))

    columns.pass_across(range(6, NZ))
    early = (0, 1)
    for j in range(RING_X):
        attend(lax.rem(h.x + order[j], RING_X))
        for tile in early:
            if j > 1:
                products.reduce(tile, j - 1)
        for tile in early:
            multiply(tile, j)
        if j == 0:
            for tile in early:
                products.reduce(tile, 0)
    for tile in early:
        products.pass_on(tile)
    for tile in early:
        products.reduce(tile, 3)
    for tile in (2, 3):
        columns.await_tile(tile)
        for j in range(RING_X):
            multiply(tile, j)
        products.reduce(tile, 0)
        if tile > 2:
            products.pass_on(tile - 1)
        products.reduce(tile, 1)
        products.reduce(tile, 2)
        products.reduce(tile, 3)
    products.pass_on(NY - 1)
    for tile in range(NY):
        products.last(tile, out)
    copies.finish()


COPIES = 2 * COPIES_A + COPIES_B + 6 + 13 + RELAY_COPIES + PRODUCT_COPIES


def rotation_tables(count):
    half_width = HD // 2
    frequency = np.float32(rope_base) ** (-np.arange(half_width, dtype=np.float32) / np.float32(half_width))
    frequency = np.concatenate([frequency, frequency]).astype(np.float64)
    inner = np.arange(count)[:, None] * frequency
    outer = (np.arange(NY * NX * NZ) * count)[:, None, None] * frequency
    return [f(angle).astype(np.float32) for angle in (inner, outer) for f in (np.cos, np.sin)]


def whole_block(doc_blocks, tokens, gain, w_query, w_key, w_value, w_out_t):
    count, width = tokens.shape
    rows = w_query.shape[0]
    half = w_query.shape[1] // 2
    near = NTP * count
    bf16 = jnp.bfloat16
    vmem = pl.BlockSpec(memory_space=pltpu.VMEM)
    turns = rotation_tables(near)
    return pl.pallas_call(
        block_kernel,
        out_shape=pltpu.VMEM((count, width), bf16),
        in_specs=[pl.BlockSpec(memory_space=pltpu.SMEM)] + [vmem] * 10,
        out_specs=vmem,
        scratch_shapes=[
            pltpu.VMEM((NX, NTP, count, width), bf16),
            pltpu.VMEM((NY, NX, NZ, rows, Q_A), bf16),
            pltpu.VMEM((NY, NX, NZ, rows, half - Q_A + HD), bf16),
            pltpu.VMEM((2, rows, half - Q_A + HD), bf16),
            pltpu.VMEM((NY, NX, NZ, rows, half), bf16),
            pltpu.VMEM((NX, NTP, half // HD * BLOCK, HD), bf16),
            pltpu.VMEM((2, NX, SPAN * near, HD), bf16),
            pltpu.VMEM((NX, SPAN * near, 2 * HD), bf16),
            pltpu.VMEM((SPAN - 1, NX, near, HD), bf16),
            pltpu.VMEM((NX, NTP, count, half), bf16),
            pltpu.VMEM((2, RING_X, 2 * NY, count, width // (2 * NY)), bf16),
            pltpu.VMEM((RING_X, 2 * NY, count, width // (2 * NY)), bf16),
            pltpu.VMEM((NY, count, width // (2 * NY)), bf16),
            pltpu.VMEM((NY, count, width // (2 * NY)), bf16),
            pltpu.VMEM((2 * NY, count, width // (2 * NY)), bf16),
            pltpu.VMEM((2 * NY, count, width // (2 * NY)), bf16),
            pltpu.VMEM((NX, near, HD), jnp.float32),
            pltpu.VMEM((NX, near, HD), jnp.float32),
            pltpu.VMEM((NX * NTP, 1, WINDOW * BLOCK), jnp.float32),
            pltpu.SemaphoreType.DMA((COPIES,)),
            pltpu.SemaphoreType.DMA((COPIES,)),
        ],
        compiler_params=pltpu.CompilerParams(
            collective_id=0, has_side_effects=True, vmem_limit_bytes=54 * 1024 * 1024
        ),
    )(doc_blocks, tokens, gain, w_query, w_key, w_value, w_out_t, *turns)


def local(tokens, norm_gain, w_query, w_key, w_value, w_out, doc_blocks):
    return whole_block(doc_blocks, tokens, norm_gain[None, :], w_query, w_key, w_value, w_out.T)


def solution(mesh):
    return jax.shard_map(
        local,
        mesh=mesh,
        in_specs=(
            P(("ctx", "tp"), None),
            P(),
            P("ctx", "tp"),
            P("ctx", "tp"),
            P("ctx", "tp"),
            P("tp", "ctx"),
            P(),
        ),
        out_specs=P(("ctx", "tp"), None),
        check_vma=False,
    )
```
